256 devices in a mesh: req: 32 (over x, z), tp: 8 (over y, core).
Axes of the slice: x: 4, y: 4, z: 8, core: 2. Of those that a mesh axis runs over, the one named last changes fastest.
Arguments:
- hidden_in: bfloat16 [32, 1024, 1024], P('req', 'tp'), may hold values from -6 to 6
- short_cache: bfloat16 [32, 1536, 2, 1024], P('req', None, None, 'tp')
- long_cache: bfloat16 [3, 16384, 2, 1024], P(None, 'req', None, 'tp')
- short_len: int32 [32], P('req'), may hold values from 512 to 1536, as said below
- long_owner: int32 [3], replicated, may hold values from 0 to 31, as said below
- w_qkv: bfloat16 [3, 1024, 1024], P(None, None, 'tp'), may hold values from -0.1875 to 0.1875
- b_qkv: float32 [3, 1024], P(None, 'tp'), may hold values from -3 to 3
- w_out: bfloat16 [1024, 1024], P('tp'), may hold values from -0.1875 to 0.1875
- b_out: float32 [1024], replicated, may hold values from -3 to 3
- w_in: bfloat16 [1024, 4096], P(None, 'tp'), may hold values from -0.1875 to 0.1875
- b_in: float32 [4096], P('tp'), may hold values from -3 to 3
- w_down: bfloat16 [4096, 1024], P('tp'), may hold values from -0.09375 to 0.09375
- b_down: float32 [1024], replicated, may hold values from -3 to 3
- norm_gain: float32 [2, 1024], replicated, may hold values from 0.1 to 1.9
- norm_offset: float32 [2, 1024], replicated, may hold values from -2 to 2
Outputs:
- hidden_out: bfloat16 [32, 1024, 1024], P('req', 'tp')
- new_kv: bfloat16 [32, 1024, 2, 1024], P('req', None, None, 'tp')
The draws below stay inside these ranges and needn't reach their ends.
Inputs may be any that keep to these rules, and one draw needn't show every extreme that they name: `short_len`: some request uses all 1536 positions. `long_owner`: 3 different requests.
All inputs are finite; a program needn't handle non-finite values.
Results may differ from the reference program's by a relative error of at most 0.025.
The reference program's roundings to bfloat16 on the way count: a program that leaves them out, or rounds other values in their place, can miss the bound.
Values may be sent and summed in bfloat16 or wider, within the bound.
A program may use at most 192 MiB of HBM per device.

```python
import jax
import jax.numpy as jnp
from jax import lax

D = 1024
HEADS = 16
HEAD_DIM = 64
FF = 4096
SPAN = 1024
SHORT_MAX = 1536
NLONG = 3
REQS = 32
LONG_LEN = 16384


def cache_values(key, shape):
    subkeys = jax.random.split(key, 1)
    is_key = (jnp.arange(2) == 0)[:, None]
    base = jax.random.normal(subkeys[0], shape, jnp.float32) * jnp.where(is_key, 2.5, 2.0)
    return base.astype(jnp.bfloat16)


def draw_short_cache(key, part):
    return cache_values(jax.random.fold_in(key, 11), (REQS, SHORT_MAX, 2, D))


def draw_long_cache(key, part):
    return cache_values(jax.random.fold_in(key, 23), (NLONG, LONG_LEN, 2, D))


def draw_short_len(key, part):
    first_key, second_key = jax.random.split(jax.random.fold_in(key, 37))
    lengths = jax.random.randint(first_key, (REQS,), SHORT_MAX // 3, SHORT_MAX + 1)
    chosen = jax.random.randint(second_key, (), 0, REQS)
    return jnp.where(jnp.arange(REQS) == chosen, SHORT_MAX, lengths).astype(jnp.int32)


def draw_long_owner(key, part):
    first_key, second_key = jax.random.split(jax.random.fold_in(key, 41))
    middle = jax.random.randint(first_key, (), 1, REQS - 1).astype(jnp.int32)
    owners = jnp.stack([jnp.zeros((), jnp.int32), jnp.full((), REQS - 1, jnp.int32), middle])
    order = jax.random.permutation(second_key, NLONG)
    return owners[order].astype(jnp.int32)


def shard_levels(key, dims, shards, smallest, largest):
    level, own = 1.0, jax.random.fold_in(key, 6)
    for axis_at, parts in shards:
        heights = jnp.exp(jax.random.uniform(jax.random.fold_in(own, axis_at), (parts,), jnp.float32, smallest / len(shards), largest / len(shards)))
        level = level * jnp.repeat(heights, dims[axis_at] // parts).reshape([-1 if axis == axis_at else 1 for axis in range(len(dims))])
    return level


def gaussian(key, dims, width, most, shards=(), kind=jnp.bfloat16):
    values = jax.random.normal(key, dims, jnp.float32) * width
    if len(shards) > 0:
        values = shard_levels(key, dims, shards, -0.22, 0.18) * values
    return jnp.clip(values, min=-most, max=most).astype(kind)


def setup_inputs(seed: int = 0) -> dict:
    keys = jax.random.split(jax.random.key(seed), 16)
    hidden_in = gaussian(keys[0], (REQS, SPAN, D), 1.0, 6.0, ((0, 32), (1, 8)))
    short_cache = draw_short_cache(jax.random.fold_in(keys[15], 71), 0)
    long_cache = draw_long_cache(jax.random.fold_in(keys[15], 71), 0)
    short_len = draw_short_len(jax.random.fold_in(keys[15], 71), 0)
    long_owner = draw_long_owner(jax.random.fold_in(keys[15], 71), 0)
    w_qkv = gaussian(keys[5], (3, D, D), D ** -0.5, 0.1875, ((2, 8),))
    b_qkv = gaussian(keys[6], (3, D), 0.5, 3.0, ((1, 8),), jnp.float32)
    w_out = gaussian(keys[7], (D, D), D ** -0.5, 0.1875, ((0, 8),))
    b_out = gaussian(keys[8], (D,), 0.5, 3.0, (), jnp.float32)
    w_in = gaussian(keys[9], (D, FF), D ** -0.5, 0.1875, ((1, 8),))
    b_in = gaussian(keys[10], (FF,), 0.5, 3.0, ((0, 8),), jnp.float32)
    w_down = gaussian(keys[11], (FF, D), FF ** -0.5, 0.09375, ((0, 8),))
    b_down = gaussian(keys[12], (D,), 0.5, 3.0, (), jnp.float32)
    norm_gain = jnp.clip(1.0 + 0.18 * jax.random.normal(keys[13], (2, D), jnp.float32), 0.1, 1.9)
    norm_offset = gaussian(keys[14], (2, D), 0.3, 2.0, (), jnp.float32)
    return dict(hidden_in=hidden_in, short_cache=short_cache, long_cache=long_cache, short_len=short_len, long_owner=long_owner, w_qkv=w_qkv, b_qkv=b_qkv, w_out=w_out, b_out=b_out, w_in=w_in, b_in=b_in, w_down=w_down, b_down=b_down, norm_gain=norm_gain, norm_offset=norm_offset)


masked_score = -1e+30

def layer_norm(rows_in, gain, shift):
    center = rows_in - lax.optimization_barrier(jnp.mean(rows_in, axis=-1, keepdims=True))
    spread = lax.optimization_barrier(jnp.mean(center * center, axis=-1, keepdims=True))
    return center * lax.rsqrt(spread + 1e-05) * gain + shift

def attend_head(query, key_matrix, value_matrix, allowed):
    logit_scores = jnp.dot(query, key_matrix.T, preferred_element_type=jnp.float32)
    logit_scores = jnp.where(allowed, logit_scores, masked_score)
    row_peak = lax.optimization_barrier(jnp.max(logit_scores, axis=1, keepdims=True))
    softmax_weights = jnp.where(allowed, jnp.exp(logit_scores - row_peak), 0.0)
    row_total = lax.optimization_barrier(jnp.sum(softmax_weights, axis=1, keepdims=True))
    summed = jnp.dot(softmax_weights.astype(jnp.bfloat16), value_matrix, preferred_element_type=jnp.float32)
    return summed / row_total

def split_heads(matrix):
    return matrix.reshape(matrix.shape[0], HEADS, HEAD_DIM).transpose(1, 0, 2)

def reference(hidden_in, short_cache, long_cache, short_len, long_owner, w_qkv, b_qkv, w_out, b_out, w_in, b_in, w_down, b_down, norm_gain, norm_offset):

    def one_request(request):
        rows_in = hidden_in[request]
        query = ((jnp.dot(rows_in, w_qkv[0], preferred_element_type=jnp.float32) + b_qkv[0]) * 0.125).astype(jnp.bfloat16)
        new_keys = (jnp.dot(rows_in, w_qkv[1], preferred_element_type=jnp.float32) + b_qkv[1]).astype(jnp.bfloat16)
        new_values = (jnp.dot(rows_in, w_qkv[2], preferred_element_type=jnp.float32) + b_qkv[2]).astype(jnp.bfloat16)
        limit = short_len[request]
        owned = long_owner == request
        has_long = jnp.any(owned)
        which_long = jnp.sum(jnp.where(owned, jnp.arange(NLONG, dtype=jnp.int32), 0)).astype(jnp.int32)
        short_rows = short_cache[request]
        causal = jnp.arange(SPAN)[None, :] <= jnp.arange(SPAN)[:, None]
        cache_mask = jnp.broadcast_to((jnp.arange(SHORT_MAX) < limit)[None, :], (SPAN, SHORT_MAX))
        base_mask = jnp.concatenate([cache_mask, causal], axis=1)
        query_heads = split_heads(query)
        base_keys = jnp.concatenate([split_heads(short_rows[:, 0]), split_heads(new_keys)], axis=1)
        base_values = jnp.concatenate([split_heads(short_rows[:, 1]), split_heads(new_values)], axis=1)

        def without_long(unused):
            return lax.map(lambda group: attend_head(group[0], group[1], group[2], base_mask), (query_heads, base_keys, base_values))

        def with_long(unused):
            long_rows = long_cache[which_long]
            all_keys = jnp.concatenate([split_heads(long_rows[:, 0]), base_keys], axis=1)
            all_values = jnp.concatenate([split_heads(long_rows[:, 1]), base_values], axis=1)
            full_mask = jnp.concatenate([jnp.ones((SPAN, LONG_LEN), bool), base_mask], axis=1)
            return lax.map(lambda group: attend_head(group[0], group[1], group[2], full_mask), (query_heads, all_keys, all_values))
        context_heads = lax.cond(has_long, with_long, without_long, 0)
        context = context_heads.transpose(1, 0, 2).reshape(SPAN, D).astype(jnp.bfloat16)
        attended = jnp.dot(context, w_out, preferred_element_type=jnp.float32) + b_out
        normed = layer_norm(rows_in.astype(jnp.float32) + attended, norm_gain[0], norm_offset[0]).astype(jnp.bfloat16)
        units = jax.nn.gelu(jnp.dot(normed, w_in, preferred_element_type=jnp.float32) + b_in, approximate=False).astype(jnp.bfloat16)
        mixed = jnp.dot(units, w_down, preferred_element_type=jnp.float32) + b_down
        hidden_out = layer_norm(normed.astype(jnp.float32) + mixed, norm_gain[1], norm_offset[1]).astype(jnp.bfloat16)
        return (hidden_out, jnp.stack([new_keys, new_values], axis=1))
    results = lax.map(one_request, jnp.arange(REQS, dtype=jnp.int32))
    return (results[0], results[1])
```

```python
import jax
import jax.numpy as jnp
from jax import lax
from jax.experimental import pallas as pl
from jax.experimental.pallas import tpu as pltpu
from jax.sharding import PartitionSpec as P

MESH = pl.DeviceIdType.MESH
F32 = jnp.float32
BF16 = jnp.bfloat16
LOW = -1e30

NREQ, NX, NZ = 32, 4, 8
NTP, NY = 8, 4
SPAN, D, WIDE = 1024, 1024, 128
SHORT, LSEG, NLONG = 1536, 512, 3
CH = 32
MSG = 48
FFH = 512


def dot(a, b):
    return jnp.dot(a, b, preferred_element_type=F32)


def dot_t(a, b):
    return lax.dot_general(a, b, (((1,), (1,)), ((), ())), preferred_element_type=F32)


def rows_of(block, size, count=None):
    return pl.ds(pl.multiple_of(block * size, size), count or size)


def kernel(
    hid_hbm, short_hbm, long_hbm, short_len, owner, wqkv_hbm, b_qkv, wout_hbm, b_out,
    win_hbm, bin_hbm, wdown_hbm, b_down, gain, offset,
    out_ref, newkv_hbm,
    hid, wq, short_raw, long_raw, wo, w1, w2, b1, q_s, k_s, v_s, kl, vl, qa, sel, qz, bias,
    spread, weave, m_st, o_st, m_l, l_l, o_l, ps, pr, merged, rs, rr, ctx, cr, nrm, part,
    own_sum, ra, rb, fl, fr, kvout,
    s_loc, s_hs, s_hr, s_ws, s_wr, s_xs, s_xr, s_es, s_er, s_qas, s_qar, s_qzs, s_qzr,
    s_ps, s_pr, s_rs, s_rr, s_cs, s_cr, s_ns, s_nr, s_fs, s_fr, s_out,
):
    me_r, me_t = lax.axis_index("req"), lax.axis_index("tp")
    y, c = me_t // 2, me_t % 2
    x, z = me_r // NZ, me_r % NZ
    yl, yr, yf = (y + 3) % 4, (y + 1) % 4, (y + 2) % 4
    right, left = (me_r, yr * 2 + c), (me_r, yl * 2 + c)
    sibling = (me_r, y * 2 + 1 - c)
    x_right, x_left = (((x + 1) % 4) * NZ + z, me_t), (((x + 3) % 4) * NZ + z, me_t)

    def remote(src, dst, ss, rs_, dev):
        return pltpu.make_async_remote_copy(
            src_ref=src, dst_ref=dst, send_sem=ss, recv_sem=rs_, device_id=dev, device_id_type=MESH
        )

    def await_bytes(ref, sem):
        pltpu.make_async_copy(ref, ref, sem).wait()

    loads = [
        (hid_hbm, hid.at[me_t]),
        (long_hbm, long_raw.at[0]),
        (short_hbm, short_raw),
        (wqkv_hbm.at[0], wq.at[:, pl.ds(0, WIDE)]),
        (wqkv_hbm.at[1], wq.at[:, pl.ds(WIDE, WIDE)]),
        (wqkv_hbm.at[2], wq.at[:, pl.ds(2 * WIDE, WIDE)]),
        (wout_hbm, wo.at[me_t]),
        (win_hbm, w1.at[c]),
        (wdown_hbm, w2.at[c]),
        (bin_hbm, b1.at[c]),
    ]
    loads = [pltpu.make_async_copy(s, d, s_loc.at[i]) for i, (s, d) in enumerate(loads)]
    for load in loads:
        load.start()

    barrier = pltpu.get_barrier_semaphore()

    @pl.loop(1, NREQ)
    def _(d):
        pl.semaphore_signal(barrier, inc=1, device_id=((me_r + d) % NREQ, me_t), device_id_type=MESH)

    @pl.loop(1, NTP)
    def _(d):
        pl.semaphore_signal(barrier, inc=1, device_id=(me_r, (me_t + d) % NTP), device_id_type=MESH)

    pl.semaphore_wait(barrier, NREQ - 1 + NTP - 1)

    def gather_start(buf, ss, sr):
        mine = buf.at[me_t]
        copies = [
            remote(mine, mine, ss.at[1], sr.at[0], right),
            remote(mine, mine, ss.at[2], sr.at[1], left),
            remote(mine, mine, ss.at[0], sr.at[4], sibling),
        ]
        for copy in copies:
            copy.start()
        return copies

    def gather_step(buf, ss, sr, step):
        if step == 1:
            slot = yl * 2 + c
            await_bytes(buf.at[slot], sr.at[0])
            half = buf.at[slot, pl.ds(0, 64)]
            copies = [
                remote(half, half, ss.at[3], sr.at[2], right),
                remote(buf.at[slot], buf.at[slot], ss.at[4], sr.at[5], sibling),
            ]
        elif step == 2:
            slot = yr * 2 + c
            await_bytes(buf.at[slot], sr.at[1])
            half = buf.at[slot, pl.ds(64, 64)]
            copies = [
                remote(half, half, ss.at[5], sr.at[3], left),
                remote(buf.at[slot], buf.at[slot], ss.at[6], sr.at[6], sibling),
            ]
        else:
            slot = yf * 2 + c
            await_bytes(buf.at[slot, pl.ds(0, 64)], sr.at[2])
            await_bytes(buf.at[slot, pl.ds(64, 64)], sr.at[3])
            copies = [remote(buf.at[slot], buf.at[slot], ss.at[7], sr.at[7], sibling)]
        for copy in copies:
            copy.start()
        return copies

    def gather_sibling(buf, sr, step):
        slot = (y, yl, yr, yf)[step] * 2 + 1 - c
        await_bytes(buf.at[slot], sr.at[4 + step])

    sent = []
    loads[0].wait()
    sent += gather_start(hid, s_hs, s_hr)
    loads[1].wait()
    x_copies = [
        remote(long_raw.at[0], long_raw.at[1], s_xs.at[0], s_xr.at[0], x_right),
        remote(long_raw.at[0], long_raw.at[2], s_xs.at[1], s_xr.at[1], x_left),
    ]
    for copy in x_copies:
        copy.start()
    sent += x_copies

    row256 = lax.broadcasted_iota(jnp.int32, (256, 256), 0)
    col256 = lax.broadcasted_iota(jnp.int32, (256, 256), 1)
    target = jnp.where(row256 < 128, 2 * row256, 2 * (row256 - 128) + 1)
    spread[...] = jnp.where(col256 == target, 1.0, 0.0).astype(BF16)
    target_t = jnp.where(col256 < 128, 2 * col256, 2 * (col256 - 128) + 1)
    weave[...] = jnp.where(row256 == target_t, 1.0, 0.0).astype(BF16)
    bias[...] = jnp.where(
        lax.broadcasted_iota(jnp.int32, (8, SHORT), 1) < short_len[0], 0.0, LOW
    )
    lane = lax.broadcasted_iota(jnp.int32, (1, WIDE), 1)
    first = jnp.where(lane < 64, 1.0, 0.0).astype(BF16)
    second = jnp.where(lane < 64, 0.0, 1.0).astype(BF16)

    def unweave(tile):
        both = dot(spread[...], tile).astype(BF16)
        return both[:128], both[128:]

    loads[2].wait()

    @pl.loop(0, 3)
    def _(g):
        for i in range(4):
            at = g * 4 + i
            keys, values = unweave(short_raw[rows_of(at, 256), :])
            k_s[rows_of(at, 128), :] = keys
            v_s[rows_of(at, 128), :] = values

    def unweave_long(slot):
        @pl.loop(0, NLONG)
        def _(j):
            for i in range(4):
                keys, values = unweave(long_raw[slot, rows_of(j * 4 + i, 256), :])
                kl[j * 4 + slot, pl.ds(i * 128, 128), :] = keys
                vl[j * 4 + slot, pl.ds(i * 128, 128), :] = values

    for i in (3, 4, 5):
        loads[i].wait()

    def project(t):
        mixed = dot(hid[t], wq[...])
        q = ((mixed[:, :WIDE] + b_qkv[0:1, :]) * 0.125).astype(BF16)
        k = (mixed[:, WIDE : 2 * WIDE] + b_qkv[1:2, :]).astype(BF16)
        v = (mixed[:, 2 * WIDE :] + b_qkv[2:3, :]).astype(BF16)
        q_s[rows_of(t, 128), :] = q
        k_s[pl.ds(pl.multiple_of(SHORT + t * 128, 128), 128), :] = k
        v_s[pl.ds(pl.multiple_of(SHORT + t * 128, 128), 128), :] = v

        @pl.loop(0, 4)
        def _(i):
            to = 4 * t + i

            @pl.when(to != me_r)
            def _():
                remote(q_s.at[rows_of(to, CH), :], qa.at[me_r], s_qas, s_qar, (to, me_t)).start()

            @pl.when(to == me_r)
            def _():
                qa[me_r] = q_s[rows_of(to, CH), :]

    project(me_t)
    gather_sibling(hid, s_hr, 0)
    project(y * 2 + 1 - c)
    unweave_long(0)
    for step, yy in ((1, yl), (2, yr), (3, yf)):
        sent += gather_step(hid, s_hs, s_hr, step)
        project(yy * 2 + c)
    for step, yy in ((1, yl), (2, yr), (3, yf)):
        gather_sibling(hid, s_hr, step)
        project(yy * 2 + 1 - c)

    for i in (6, 7, 8, 9):
        loads[i].wait()
    sent += gather_start(wo, s_ws, s_wr)
    swap = [
        remote(w1.at[c], w1.at[c], s_es.at[0], s_er.at[0], sibling),
        remote(w2.at[c], w2.at[c], s_es.at[1], s_er.at[1], sibling),
        remote(b1.at[c], b1.at[c], s_es.at[2], s_er.at[2], sibling),
    ]
    for copy in swap:
        copy.start()
    sent += swap

    def attend_init():
        m_st[...] = jnp.full(m_st.shape, LOW, F32)
        o_st[...] = jnp.zeros(o_st.shape, F32)

    def attend_step(q, k, v, extra):
        vs = (v * first + second, v * second + first)
        for h, mask in enumerate((first, second)):
            s = dot_t(q * mask, k)
            if extra is not None:
                s = s + extra
            m_old = m_st[h]
            m_new = jnp.maximum(m_old, jnp.max(s, axis=1, keepdims=True))
            wide = jnp.concatenate([m_new] * (s.shape[1] // WIDE), axis=1)
            p = jnp.exp(s - wide).astype(BF16)
            o_st[h] = o_st[h] * jnp.exp(m_old - m_new) + dot(p, vs[h])
            m_st[h] = m_new

    def attend_end():
        low = lax.broadcasted_iota(jnp.int32, (256, WIDE), 1) < 64
        total = pltpu.roll(jnp.where(low, o_st[1], o_st[0]), 64, 1)
        return jnp.where(low, m_st[0], m_st[1]), total, jnp.where(low, o_st[0], o_st[1])

    def attend_local(b):
        q = q_s[rows_of(b, 256), :]
        attend_init()

        @pl.loop(0, 3)
        def _(i):
            at = rows_of(i, 512)
            attend_step(q, k_s[at, :], v_s[at, :], bias[0:1, at])

        @pl.loop(0, b)
        def _(i):
            at = pl.ds(pl.multiple_of(SHORT + i * 256, 256), 256)
            attend_step(q, k_s[at, :], v_s[at, :], None)

        at = pl.ds(pl.multiple_of(SHORT + b * 256, 256), 256)
        attend_step(q, k_s[at, :], v_s[at, :], jnp.where(col256 <= row256, 0.0, LOW))
        m, total, o = attend_end()
        m_l[rows_of(b, 256), :] = m
        l_l[rows_of(b, 256), :] = total
        o_l[rows_of(b, 256), :] = o

    lane32 = lax.broadcasted_iota(jnp.int32, (CH, WIDE), 1) % 64
    diagonal = jnp.where(lane32 == lax.broadcasted_iota(jnp.int32, (CH, WIDE), 0), 1.0, 0.0)
    tile_row = lax.broadcasted_iota(jnp.int32, (16, WIDE), 0)
    side_r = lax.broadcasted_iota(jnp.int32, (WIDE, WIDE), 0) // 64
    side_c = lax.broadcasted_iota(jnp.int32, (WIDE, WIDE), 1) // 64
    sides = jnp.where(side_r == side_c, 1.0, 0.0).astype(BF16)

    def pack_stats(lse):
        row = jnp.sum(lse * diagonal, axis=0, keepdims=True)
        hi = row.astype(BF16).astype(F32)
        mid = (row - hi).astype(BF16).astype(F32)
        lo = row - hi - mid
        tile = jnp.where(tile_row == 0, hi, jnp.where(tile_row == 1, mid, jnp.where(tile_row == 2, lo, 0.0)))
        return tile.astype(BF16)

    def unpack_stats(tiles):
        n = tiles.shape[0]
        tiles = tiles.astype(F32)
        lse = None
        for i in range(3):
            spread_out = tiles[:, i : i + 1, :] * diagonal[None]
            term = dot(spread_out.reshape(n * CH, WIDE).astype(BF16), sides)
            lse = term if lse is None else lse + term
        return lse

    @pl.loop(0, 2)
    def _(b):
        attend_local(b)

    await_bytes(qa.at[pl.ds(0, NREQ - 1)], s_qar)
    for j in range(NLONG):
        sel[j] = qa[owner[j]]
    qz[0] = sel[...]

    @pl.loop(1, NZ)
    def _(d):
        to = x * NZ + (z + d) % NZ
        remote(sel, qz.at[d], s_qzs, s_qzr, (to, me_t)).start()

    await_bytes(long_raw.at[1], s_xr.at[0])
    half = pl.ds(0, SHORT)
    copy = remote(long_raw.at[1, half], long_raw.at[3, half], s_xs.at[2], s_xr.at[2], x_right)
    copy.start()
    sent.append(copy)
    await_bytes(long_raw.at[2], s_xr.at[1])
    half = pl.ds(SHORT, SHORT)
    copy = remote(long_raw.at[2, half], long_raw.at[3, half], s_xs.at[3], s_xr.at[3], x_left)
    copy.start()
    sent.append(copy)
    for step in (1, 2):
        sent += gather_step(wo, s_ws, s_wr, step)
    unweave_long(1)
    unweave_long(2)

    attend_local(2)
    sent += gather_step(wo, s_ws, s_wr, 3)

    await_bytes(long_raw.at[3, pl.ds(0, SHORT)], s_xr.at[2])
    await_bytes(long_raw.at[3, pl.ds(SHORT, SHORT)], s_xr.at[3])
    unweave_long(3)
    await_bytes(qz.at[pl.ds(1, NZ - 1)], s_qzr)

    @pl.loop(0, NLONG)
    def _(j):
        q = qz[:, j].reshape(256, WIDE)
        attend_init()

        @pl.loop(0, NX)
        def _(i):
            attend_step(q, kl[j * 4 + i], vl[j * 4 + i], None)

        m, total, o = attend_end()
        lse = m + jnp.log(total)
        o = (o / total).astype(BF16)
        for d in range(NZ):
            at = slice(d * CH, (d + 1) * CH)
            dst = pr if d == 0 else ps
            dst[j, d, 0:CH] = o[at]
            dst[j, d, CH:MSG] = pack_stats(lse[at])

        @pl.loop(1, NZ)
        def _(d):
            to = x * NZ + (z + NZ - d) % NZ
            remote(ps.at[j, d], pr.at[j, d], s_ps.at[j], s_pr.at[j], (to, me_t)).start()

    attend_local(3)

    @pl.loop(0, NLONG)
    def _(j):
        await_bytes(pr.at[j, pl.ds(1, NZ - 1)], s_pr.at[j])
        lse = unpack_stats(pr[j, :, CH:MSG]).reshape(NZ, CH, WIDE)
        top = jnp.max(lse, axis=0, keepdims=True)
        w = jnp.exp(lse - top)
        total = jnp.sum(w, axis=0)
        o = jnp.sum(w * pr[j, :, 0:CH].astype(F32), axis=0) / total
        merged[j, 0:CH] = o
        merged[j, CH:MSG] = pack_stats(top[0] + jnp.log(total)).astype(F32)

    msg_row = lax.broadcasted_iota(jnp.int32, (MSG, WIDE), 0)
    empty = jnp.where(msg_row == CH, LOW, 0.0)

    @pl.loop(0, NREQ)
    def _(r):
        value, rest = None, 1.0
        for j in range(NLONG):
            mine = jnp.where(owner[j] == r, 1.0, 0.0)
            term = merged[j] * mine
            value = term if value is None else value + term
            rest = rest - mine
        message = (value + empty * rest).astype(BF16)

        @pl.when(r == me_r)
        def _():
            rr[me_r] = message

        @pl.when(r != me_r)
        def _():
            rs[r] = message
            remote(rs.at[r], rr.at[me_r], s_rs, s_rr, (r, me_t)).start()

    @pl.loop(0, 4)
    def _(g):
        for i in range(2):
            t = g * 2 + i
            at = pl.ds(pl.multiple_of(SHORT + t * 128, 128), 128)
            both = jnp.concatenate([k_s[at, :], v_s[at, :]], axis=0)
            kvout[rows_of(t, 256), :] = dot(weave[...], both).astype(BF16)

    out_copy = pltpu.make_async_copy(kvout, newkv_hbm, s_out.at[0])
    out_copy.start()

    await_bytes(rr.at[pl.ds(0, NREQ - 1)], s_rr)

    @pl.loop(0, 4)
    def _(b):
        at = rows_of(b, 256)
        msgs = rr[pl.ds(b * 8, 8)]
        lse = unpack_stats(msgs[:, CH:MSG])
        o = msgs[:, 0:CH].astype(F32).reshape(256, WIDE)
        m = m_l[at, :]
        top = jnp.maximum(m, lse)
        a, w = jnp.exp(m - top), jnp.exp(lse - top)
        value = (o_l[at, :] * a + o * w) / (l_l[at, :] * a + w)
        ctx[at, :] = value.astype(BF16)
        for i in range(2):
            to = b * 2 + i

            @pl.when(to != me_t)
            def _():
                remote(ctx.at[rows_of(to, 128), :], cr.at[me_t], s_cs, s_cr, (me_r, to)).start()

            @pl.when(to == me_t)
            def _():
                cr[me_t] = ctx[rows_of(to, 128), :]

    for step in range(4):
        gather_sibling(wo, s_wr, step)
    await_bytes(cr.at[pl.ds(0, NTP - 1)], s_cr)
    attended = b_out[...]
    for h in range(NTP):
        attended = attended + dot(cr[h], wo[h])

    def norm(rows, which):
        center = rows - jnp.mean(rows, axis=-1, keepdims=True)
        var = jnp.mean(center * center, axis=-1, keepdims=True)
        return (center * lax.rsqrt(var + 1e-5) * gain[which : which + 1, :] + offset[which : which + 1, :]).astype(BF16)

    nrm[0] = norm(hid[me_t].astype(F32) + attended, 0)

    copies = [
        remote(nrm.at[0], nrm.at[1], s_ns.at[0], s_nr.at[0], right),
        remote(nrm.at[0], nrm.at[2], s_ns.at[1], s_nr.at[1], left),
    ]
    for copy in copies:
        copy.start()
    sent += copies
    await_bytes(w1.at[1 - c], s_er.at[0])
    await_bytes(w2.at[1 - c], s_er.at[1])
    await_bytes(b1.at[1 - c], s_er.at[2])

    def feed(slot):
        rows = nrm[slot]
        total = None
        for i in range(2):
            u = dot(rows, w1[i]) + b1[i]
            u = (0.5 * u * (1.0 + lax.erf(u * 0.7071067811865476))).astype(BF16)
            term = dot(u, w2[i])
            total = term if total is None else total + term
        return total

    def start(*args):
        copy = remote(*args)
        copy.start()
        sent.append(copy)

    top_half, low_half = pl.ds(0, 64), pl.ds(64, 64)
    own_sum[...] = feed(0)
    await_bytes(nrm.at[1], s_nr.at[0])
    start(nrm.at[1, top_half], nrm.at[3, top_half], s_ns.at[2], s_nr.at[2], right)
    await_bytes(nrm.at[2], s_nr.at[1])
    start(nrm.at[2, low_half], nrm.at[3, low_half], s_ns.at[3], s_nr.at[3], left)
    part[1] = feed(1).astype(BF16)
    start(part.at[1, top_half], fr.at[top_half], s_fs.at[0], s_fr.at[0], left)
    part[2] = feed(2).astype(BF16)
    start(part.at[2, low_half], fl.at[low_half], s_fs.at[1], s_fr.at[1], right)
    await_bytes(nrm.at[3, top_half], s_nr.at[2])
    await_bytes(nrm.at[3, low_half], s_nr.at[3])
    part[3] = feed(3).astype(BF16)
    start(part.at[3, top_half], ra, s_fs.at[2], s_fr.at[2], right)
    start(part.at[3, low_half], rb, s_fs.at[3], s_fr.at[3], left)
    await_bytes(ra, s_fr.at[2])
    part[2, 0:64] = (part[2, 0:64].astype(F32) + ra[...].astype(F32)).astype(BF16)
    start(part.at[2, top_half], fl.at[top_half], s_fs.at[4], s_fr.at[4], right)
    await_bytes(rb, s_fr.at[3])
    part[1, 64:128] = (part[1, 64:128].astype(F32) + rb[...].astype(F32)).astype(BF16)
    start(part.at[1, low_half], fr.at[low_half], s_fs.at[5], s_fr.at[5], left)
    await_bytes(fr.at[top_half], s_fr.at[0])
    await_bytes(fl.at[low_half], s_fr.at[1])
    await_bytes(fl.at[top_half], s_fr.at[4])
    await_bytes(fr.at[low_half], s_fr.at[5])
    mixed = own_sum[...] + fl[...].astype(F32) + fr[...].astype(F32) + b_down[...]
    out_ref[...] = norm(nrm[0].astype(F32) + mixed, 1)

    for copy in sent:
        copy.wait_send()
    await_bytes(qa.at[pl.ds(0, NREQ - 1)], s_qas)
    await_bytes(qz.at[pl.ds(1, NZ - 1)], s_qzs)
    for j in range(NLONG):
        await_bytes(pr.at[j, pl.ds(1, NZ - 1)], s_ps.at[j])
    await_bytes(rr.at[pl.ds(0, NREQ - 1)], s_rs)
    await_bytes(cr.at[pl.ds(0, NTP - 1)], s_cs)
    out_copy.wait()


def body(
    hidden_in, short_cache, long_cache, short_len, long_owner, w_qkv, b_qkv, w_out, b_out,
    w_in, b_in, w_down, b_down, norm_gain, norm_offset,
):
    hbm = pl.BlockSpec(memory_space=pl.ANY)
    vmem = pl.BlockSpec(memory_space=pltpu.VMEM)
    smem = pl.BlockSpec(memory_space=pltpu.SMEM)
    V, S = pltpu.VMEM, pltpu.SemaphoreType.DMA
    hidden_out, new_kv = pl.pallas_call(
        kernel,
        out_shape=(
            jax.ShapeDtypeStruct((128, D), BF16),
            jax.ShapeDtypeStruct((2 * SPAN, WIDE), BF16),
        ),
        in_specs=[
            hbm, hbm, hbm, smem, smem, hbm, vmem, hbm, vmem, hbm, hbm, hbm, vmem, vmem, vmem,
        ],
        out_specs=(vmem, hbm),
        scratch_shapes=[
            V((NTP, 128, D), BF16),
            V((D, 3 * WIDE), BF16),
            V((2 * SHORT, WIDE), BF16),
            V((NX, 2 * NLONG * LSEG, WIDE), BF16),
            V((NTP, WIDE, D), BF16),
            V((2, D, FFH), BF16),
            V((2, FFH, D), BF16),
            V((2, 1, FFH), F32),
            V((SPAN, WIDE), BF16),
            V((SHORT + SPAN, WIDE), BF16),
            V((SHORT + SPAN, WIDE), BF16),
            V((NLONG * NX, LSEG, WIDE), BF16),
            V((NLONG * NX, LSEG, WIDE), BF16),
            V((NREQ, CH, WIDE), BF16),
            V((NLONG, CH, WIDE), BF16),
            V((NZ, NLONG, CH, WIDE), BF16),
            V((8, SHORT), F32),
            V((256, 256), BF16),
            V((256, 256), BF16),
            V((2, 256, WIDE), F32),
            V((2, 256, WIDE), F32),
            V((SPAN, WIDE), F32),
            V((SPAN, WIDE), F32),
            V((SPAN, WIDE), F32),
            V((NLONG, NZ, MSG, WIDE), BF16),
            V((NLONG, NZ, MSG, WIDE), BF16),
            V((NLONG, MSG, WIDE), F32),
            V((NREQ, MSG, WIDE), BF16),
            V((NREQ, MSG, WIDE), BF16),
            V((SPAN, WIDE), BF16),
            V((NTP, 128, WIDE), BF16),
            V((NY, 128, D), BF16),
            V((NY, 128, D), BF16),
            V((128, D), F32),
            V((64, D), BF16),
            V((64, D), BF16),
            V((128, D), BF16),
            V((128, D), BF16),
            V((2 * SPAN, WIDE), BF16),
            S((10,)), S((8,)), S((8,)), S((8,)), S((8,)), S((4,)), S((4,)), S((3,)), S((3,)),
            S, S, S, S, S((3,)), S((3,)), S, S, S, S, S((4,)), S((4,)), S((6,)), S((6,)), S((1,)),
        ],
        compiler_params=pltpu.CompilerParams(
            collective_id=0, has_side_effects=True, vmem_limit_bytes=56 * 1024 * 1024
        ),
    )(
        hidden_in[0],
        short_cache.reshape(2 * SHORT, WIDE),
        long_cache.reshape(2 * NLONG * LSEG, WIDE),
        short_len,
        long_owner,
        w_qkv,
        b_qkv,
        w_out,
        b_out[None],
        w_in,
        b_in[None],
        w_down,
        b_down[None],
        norm_gain,
        norm_offset,
    )
    return (hidden_out[None], new_kv.reshape(1, SPAN, 2, WIDE))


def solution(mesh):
    return jax.shard_map(
        body,
        mesh=mesh,
        in_specs=(
            P("req", "tp", None),
            P("req", None, None, "tp"),
            P(None, "req", None, "tp"),
            P("req"),
            P(),
            P(None, None, "tp"),
            P(None, "tp"),
            P("tp", None),
            P(),
            P(None, "tp"),
            P("tp"),
            P("tp", None),
            P(),
            P(),
            P(),
        ),
        out_specs=(P("req", "tp", None), P("req", None, None, "tp")),
        check_vma=False,
    )
```

```python
import jax
import jax.numpy as jnp
from jax import lax
from jax.experimental import pallas as pl
from jax.experimental.pallas import tpu as pltpu
from jax.sharding import PartitionSpec as P

MESH = pl.DeviceIdType.MESH
F32 = jnp.float32
BF16 = jnp.bfloat16
LOW = -1e30

NREQ, NX, NZ = 32, 4, 8
NTP, NY = 8, 4
SPAN, D, WIDE = 1024, 1024, 128
SHORT, LSEG, NLONG = 1536, 512, 3
CH = 32
MSG = 48
FFH = 512


def dot(a, b):
    return jnp.dot(a, b, preferred_element_type=F32)


def dot_t(a, b):
    return lax.dot_general(a, b, (((1,), (1,)), ((), ())), preferred_element_type=F32)


def rows_of(block, size, count=None):
    return pl.ds(pl.multiple_of(block * size, size), count or size)


def kernel(
    hid_hbm, short_hbm, long_hbm, short_len, owner, wqkv_hbm, b_qkv, wout_hbm, b_out,
    win_hbm, bin_hbm, wdown_hbm, b_down, gain, offset,
    out_ref, newkv_hbm,
    hid, wq, short_raw, long_raw, wo, w1, w2, b1, q_s, k_s, v_s, kl, vl, qa, sel, qz, bias,
    spread, weave, m_s, o_s, m_g, o_g, m_l, l_l, o_l, ps, pr, merged, rs, rr, ctx, cr, nrm, part,
    own_sum, ra, rb, fl, fr, kvout,
    s_loc, s_hs, s_hr, s_ws, s_wr, s_xs, s_xr, s_es, s_er, s_qas, s_qar, s_qzs, s_qzr,
    s_ps, s_pr, s_rs, s_rr, s_cs, s_cr, s_ns, s_nr, s_fs, s_fr, s_out,
):
    me_r, me_t = lax.axis_index("req"), lax.axis_index("tp")
    y, c = me_t // 2, me_t % 2
    x, z = me_r // NZ, me_r % NZ
    yl, yr, yf = (y + 3) % 4, (y + 1) % 4, (y + 2) % 4
    right, left = (me_r, yr * 2 + c), (me_r, yl * 2 + c)
    sibling = (me_r, y * 2 + 1 - c)
    right_other, left_other = (me_r, yr * 2 + 1 - c), (me_r, yl * 2 + 1 - c)
    x_right, x_left = (((x + 1) % 4) * NZ + z, me_t), (((x + 3) % 4) * NZ + z, me_t)

    def remote(src, dst, ss, rs_, dev):
        return pltpu.make_async_remote_copy(
            src_ref=src, dst_ref=dst, send_sem=ss, recv_sem=rs_, device_id=dev, device_id_type=MESH
        )

    def await_bytes(ref, sem):
        pltpu.make_async_copy(ref, ref, sem).wait()

    loads = [
        (hid_hbm, hid.at[me_t]),
        (long_hbm, long_raw.at[0]),
        (short_hbm, short_raw),
        (wqkv_hbm.at[0], wq.at[:, pl.ds(0, WIDE)]),
        (wqkv_hbm.at[1], wq.at[:, pl.ds(WIDE, WIDE)]),
        (wqkv_hbm.at[2], wq.at[:, pl.ds(2 * WIDE, WIDE)]),
        (wout_hbm, wo.at[me_t]),
        (win_hbm, w1.at[c]),
        (wdown_hbm, w2.at[c]),
        (bin_hbm, b1.at[c]),
    ]
    loads = [pltpu.make_async_copy(s, d, s_loc.at[i]) for i, (s, d) in enumerate(loads)]
    for load in loads:
        load.start()

    barrier = pltpu.get_barrier_semaphore()

    @pl.loop(1, NREQ)
    def _(d):
        pl.semaphore_signal(barrier, inc=1, device_id=((me_r + d) % NREQ, me_t), device_id_type=MESH)

    @pl.loop(1, NTP)
    def _(d):
        pl.semaphore_signal(barrier, inc=1, device_id=(me_r, (me_t + d) % NTP), device_id_type=MESH)

    pl.semaphore_wait(barrier, NREQ - 1 + NTP - 1)

    top_half, low_half = pl.ds(0, 64), pl.ds(64, 64)

    def begin(*args):
        copy = remote(*args)
        copy.start()
        sent.append(copy)

    def gather_start(buf, ss, sr):
        mine, top, low = buf.at[me_t], buf.at[me_t, top_half], buf.at[me_t, low_half]
        begin(top, top, ss.at[1], sr.at[0], right)
        begin(low, low, ss.at[2], sr.at[2], left)
        begin(top, top, ss.at[10], sr.at[10], right_other)
        begin(low, low, ss.at[11], sr.at[11], left_other)
        begin(low, low, ss.at[3], sr.at[1], right)
        begin(top, top, ss.at[4], sr.at[3], left)
        begin(mine, mine, ss.at[0], sr.at[6], sibling)

    def gather_forward(buf, ss, sr):
        half = buf.at[yl * 2 + c, top_half]
        await_bytes(half, sr.at[0])
        begin(half, half, ss.at[5], sr.at[4], right)
        half = buf.at[yr * 2 + c, low_half]
        await_bytes(half, sr.at[2])
        begin(half, half, ss.at[6], sr.at[5], left)

    def gather_share(buf, ss, sr, step):
        slot = (y, yl, yr, yf)[step] * 2 + c
        if step == 1:
            await_bytes(buf.at[slot, low_half], sr.at[1])
        elif step == 2:
            await_bytes(buf.at[slot, top_half], sr.at[3])
        else:
            await_bytes(buf.at[slot, top_half], sr.at[4])
            await_bytes(buf.at[slot, low_half], sr.at[5])
        share = buf.at[slot] if step == 3 else buf.at[slot, (None, low_half, top_half)[step]]
        begin(share, share, ss.at[6 + step], sr.at[6 + step], sibling)

    def gather_sibling(buf, sr, step):
        slot = (y, yl, yr, yf)[step] * 2 + 1 - c
        if step == 1:
            await_bytes(buf.at[slot, top_half], sr.at[10])
            await_bytes(buf.at[slot, low_half], sr.at[7])
        elif step == 2:
            await_bytes(buf.at[slot, low_half], sr.at[11])
            await_bytes(buf.at[slot, top_half], sr.at[8])
        else:
            await_bytes(buf.at[slot], sr.at[6 + step])

    sent = []
    loads[0].wait()
    gather_start(hid, s_hs, s_hr)
    loads[1].wait()

    def x_rows(j, half=None):
        if half is None:
            return rows_of(j, 2 * LSEG)
        return pl.ds(pl.multiple_of(j * 2 * LSEG + half * LSEG, LSEG), LSEG)

    def x_send(j):
        own = long_raw.at[0, x_rows(j)]
        begin(own, long_raw.at[1, x_rows(j)], s_xs.at[4 * j], s_xr.at[4 * j], x_right)
        begin(own, long_raw.at[2, x_rows(j)], s_xs.at[4 * j + 1], s_xr.at[4 * j + 1], x_left)

    def x_forward(j):
        for half, to in ((0, x_right), (1, x_left)):
            await_bytes(long_raw.at[1 + half, x_rows(j)], s_xr.at[4 * j + half])
            at, k = x_rows(j, half), 4 * j + 2 + half
            begin(long_raw.at[1 + half, at], long_raw.at[3, at], s_xs.at[k], s_xr.at[k], to)

    x_send(0)
    x_send(1)

    row256 = lax.broadcasted_iota(jnp.int32, (256, 256), 0)
    col256 = lax.broadcasted_iota(jnp.int32, (256, 256), 1)
    target = jnp.where(row256 < 128, 2 * row256, 2 * (row256 - 128) + 1)
    spread[...] = jnp.where(col256 == target, 1.0, 0.0).astype(BF16)
    target_t = jnp.where(col256 < 128, 2 * col256, 2 * (col256 - 128) + 1)
    weave[...] = jnp.where(row256 == target_t, 1.0, 0.0).astype(BF16)
    bias[...] = jnp.where(
        lax.broadcasted_iota(jnp.int32, (8, SHORT), 1) < short_len[0], 0.0, LOW
    )
    lane = lax.broadcasted_iota(jnp.int32, (1, WIDE), 1)
    first = jnp.where(lane < 64, 1.0, 0.0).astype(BF16)
    second = jnp.where(lane < 64, 0.0, 1.0).astype(BF16)

    def unweave(tile):
        both = dot(spread[...], tile).astype(BF16)
        return both[:128], both[128:]

    loads[2].wait()

    @pl.loop(0, 3)
    def _(g):
        for i in range(4):
            at = g * 4 + i
            keys, values = unweave(short_raw[rows_of(at, 256), :])
            k_s[rows_of(at, 128), :] = keys
            v_s[rows_of(at, 128), :] = values

    def unweave_long(j, slot):
        for i in range(4):
            keys, values = unweave(long_raw[slot, rows_of(j * 4 + i, 256), :])
            at = pl.ds(slot * LSEG + i * 128, 128)
            kl[j, at, :] = keys
            vl[j, at, :] = values

    for i in (3, 4, 5):
        loads[i].wait()

    def project(t):
        mixed = dot(hid[t], wq[...])
        q = ((mixed[:, :WIDE] + b_qkv[0:1, :]) * 0.125).astype(BF16)
        k = (mixed[:, WIDE : 2 * WIDE] + b_qkv[1:2, :]).astype(BF16)
        v = (mixed[:, 2 * WIDE :] + b_qkv[2:3, :]).astype(BF16)
        q_s[rows_of(t, 128), :] = q
        k_s[pl.ds(pl.multiple_of(SHORT + t * 128, 128), 128), :] = k
        v_s[pl.ds(pl.multiple_of(SHORT + t * 128, 128), 128), :] = v

        @pl.loop(0, 4)
        def _(i):
            to = 4 * t + i

            @pl.when(to != me_r)
            def _():
                remote(q_s.at[rows_of(to, CH), :], qa.at[me_r], s_qas, s_qar, (to, me_t)).start()

            @pl.when(to == me_r)
            def _():
                qa[me_r] = q_s[rows_of(to, CH), :]

    def attend(q, k, v, extra, m_ref, o_ref, fresh):
        vs = (v * first + second, v * second + first)
        scores = [dot_t(q * mask, k) for mask in (first, second)]
        for h, s in enumerate(scores):
            if extra is not None:
                s = extra(s)
            m_new = jnp.max(s, axis=1, keepdims=True)
            if fresh:
                m_new = jnp.broadcast_to(m_new, (256, WIDE))
            else:
                m_old = m_ref[h]
                m_new = jnp.maximum(m_old, m_new)
            wide = jnp.concatenate([m_new] * (s.shape[1] // WIDE), axis=1)
            o = dot(jnp.exp(s - wide).astype(BF16), vs[h])
            o_ref[h] = o if fresh else o_ref[h] * jnp.exp(m_old - m_new) + o
            m_ref[h] = m_new

    def attend_end(m_ref, o_ref):
        low = lax.broadcasted_iota(jnp.int32, (256, WIDE), 1) < 64
        total = pltpu.roll(jnp.where(low, o_ref[1], o_ref[0]), 64, 1)
        return jnp.where(low, m_ref[0], m_ref[1]), total, jnp.where(low, o_ref[0], o_ref[1])

    m_s[...] = jnp.full(m_s.shape, LOW, F32)
    o_s[...] = jnp.zeros(o_s.shape, F32)

    def attend_short(b):
        attend(
            q_s[rows_of(b, 256), :], k_s[:SHORT, :], v_s[:SHORT, :], lambda s: s + bias[0:1, :],
            m_s.at[b], o_s.at[b], False,
        )

    def attend_new(b):
        at = slice(SHORT, SHORT + 256 * (b + 1))
        causal = jnp.where(col256 <= row256, 0.0, LOW)

        def extra(s):
            last = s[:, 256 * b :] + causal
            return jnp.concatenate([s[:, : 256 * b], last], axis=1) if b else last

        attend(q_s[b * 256 : (b + 1) * 256, :], k_s[at, :], v_s[at, :], extra, m_s.at[b], o_s.at[b], False)

    def attend_local_end(b):
        m, total, o = attend_end(m_s.at[b], o_s.at[b])
        m_l[rows_of(b, 256), :] = m
        l_l[rows_of(b, 256), :] = total
        o_l[rows_of(b, 256), :] = o

    project(me_t)
    gather_sibling(hid, s_hr, 0)
    project(y * 2 + 1 - c)
    attend_short(y)
    gather_forward(hid, s_hs, s_hr)
    gather_share(hid, s_hs, s_hr, 1)
    project(yl * 2 + c)
    gather_share(hid, s_hs, s_hr, 2)
    project(yr * 2 + c)
    gather_sibling(hid, s_hr, 1)
    project(yl * 2 + 1 - c)
    x_forward(0)
    gather_share(hid, s_hs, s_hr, 3)
    project(yf * 2 + c)
    gather_sibling(hid, s_hr, 2)
    project(yr * 2 + 1 - c)
    gather_sibling(hid, s_hr, 3)
    project(yf * 2 + 1 - c)

    for i in (6, 7, 8, 9):
        loads[i].wait()
    gather_start(wo, s_ws, s_wr)
    begin(w1.at[c], w1.at[c], s_es.at[0], s_er.at[0], sibling)
    begin(w2.at[c], w2.at[c], s_es.at[1], s_er.at[1], sibling)
    begin(b1.at[c], b1.at[c], s_es.at[2], s_er.at[2], sibling)
    x_forward(1)
    for j in range(NLONG):
        unweave_long(j, 0)
    attend_short(yl)

    lane32 = lax.broadcasted_iota(jnp.int32, (CH, WIDE), 1) % 64
    diagonal = jnp.where(lane32 == lax.broadcasted_iota(jnp.int32, (CH, WIDE), 0), 1.0, 0.0)
    tile_row = lax.broadcasted_iota(jnp.int32, (16, WIDE), 0)
    side_r = lax.broadcasted_iota(jnp.int32, (WIDE, WIDE), 0) // 64
    side_c = lax.broadcasted_iota(jnp.int32, (WIDE, WIDE), 1) // 64
    sides = jnp.where(side_r == side_c, 1.0, 0.0).astype(BF16)

    def pack_stats(lse):
        row = jnp.sum(lse * diagonal, axis=0, keepdims=True)
        hi = row.astype(BF16).astype(F32)
        mid = (row - hi).astype(BF16).astype(F32)
        lo = row - hi - mid
        tile = jnp.where(tile_row == 0, hi, jnp.where(tile_row == 1, mid, jnp.where(tile_row == 2, lo, 0.0)))
        return tile.astype(BF16)

    def unpack_stats(tiles):
        n = tiles.shape[0]
        tiles = tiles.astype(F32)
        lse = None
        for i in range(3):
            spread_out = tiles[:, i : i + 1, :] * diagonal[None]
            term = dot(spread_out.reshape(n * CH, WIDE).astype(BF16), sides)
            lse = term if lse is None else lse + term
        return lse

    await_bytes(qa.at[pl.ds(0, NREQ - 1)], s_qar)
    for j in range(NLONG):
        sel[j] = qa[owner[j]]
    qz[0] = sel[...]

    @pl.loop(1, NZ)
    def _(d):
        to = x * NZ + (z + d) % NZ
        remote(sel, qz.at[d], s_qzs, s_qzr, (to, me_t)).start()

    x_send(2)

    @pl.loop(0, 4)
    def _(g):
        for i in range(2):
            t = g * 2 + i
            at = pl.ds(pl.multiple_of(SHORT + t * 128, 128), 128)
            both = jnp.concatenate([k_s[at, :], v_s[at, :]], axis=0)
            kvout[rows_of(t, 256), :] = dot(weave[...], both).astype(BF16)

    out_copy = pltpu.make_async_copy(kvout, newkv_hbm, s_out.at[0])
    out_copy.start()
    gather_forward(wo, s_ws, s_wr)
    attend_new(0)
    attend_new(1)
    for j in range(2):
        unweave_long(j, 1)
        unweave_long(j, 2)
    x_forward(2)
    unweave_long(2, 1)
    unweave_long(2, 2)
    for step in (1, 2, 3):
        gather_share(wo, s_ws, s_wr, step)
    await_bytes(qz.at[pl.ds(1, NZ - 1)], s_qzr)

    @pl.loop(0, NLONG)
    def _(j):
        for half in range(2):
            await_bytes(long_raw.at[3, x_rows(j, half)], s_xr.at[4 * j + 2 + half])
        unweave_long(j, 3)
        attend(qz[:, j].reshape(256, WIDE), kl[j], vl[j], None, m_g, o_g, True)
        m, total, o = attend_end(m_g, o_g)
        lse = m + jnp.log(total)
        o = (o / total).astype(BF16)
        for d in range(NZ):
            at = slice(d * CH, (d + 1) * CH)
            dst = pr if d == 0 else ps
            dst[j, d, 0:CH] = o[at]
            dst[j, d, CH:MSG] = pack_stats(lse[at])

        @pl.loop(1, NZ)
        def _(d):
            to = x * NZ + (z + NZ - d) % NZ
            remote(ps.at[j, d], pr.at[j, d], s_ps.at[j], s_pr.at[j], (to, me_t)).start()

    attend_short(yr)
    attend_new(2)

    @pl.loop(0, NLONG)
    def _(j):
        await_bytes(pr.at[j, pl.ds(1, NZ - 1)], s_pr.at[j])
        lse = unpack_stats(pr[j, :, CH:MSG]).reshape(NZ, CH, WIDE)
        top = jnp.max(lse, axis=0, keepdims=True)
        w = jnp.exp(lse - top)
        total = jnp.sum(w, axis=0)
        o = jnp.sum(w * pr[j, :, 0:CH].astype(F32), axis=0) / total
        merged[j, 0:CH] = o
        merged[j, CH:MSG] = pack_stats(top[0] + jnp.log(total)).astype(F32)

    msg_row = lax.broadcasted_iota(jnp.int32, (MSG, WIDE), 0)
    empty = jnp.where(msg_row == CH, LOW, 0.0)

    @pl.loop(0, NREQ)
    def _(r):
        value, rest = None, 1.0
        for j in range(NLONG):
            mine = jnp.where(owner[j] == r, 1.0, 0.0)
            term = merged[j] * mine
            value = term if value is None else value + term
            rest = rest - mine
        message = (value + empty * rest).astype(BF16)

        @pl.when(r == me_r)
        def _():
            rr[me_r] = message

        @pl.when(r != me_r)
        def _():
            rs[r] = message
            remote(rs.at[r], rr.at[me_r], s_rs, s_rr, (r, me_t)).start()

    attend_short(yf)
    attend_new(3)
    for b in range(4):
        attend_local_end(b)

    await_bytes(rr.at[pl.ds(0, NREQ - 1)], s_rr)

    @pl.loop(0, 4)
    def _(b):
        at = rows_of(b, 256)
        msgs = rr[pl.ds(b * 8, 8)]
        lse = unpack_stats(msgs[:, CH:MSG])
        o = msgs[:, 0:CH].astype(F32).reshape(256, WIDE)
        m = m_l[at, :]
        top = jnp.maximum(m, lse)
        a, w = jnp.exp(m - top), jnp.exp(lse - top)
        value = (o_l[at, :] * a + o * w) / (l_l[at, :] * a + w)
        ctx[at, :] = value.astype(BF16)
        for i in range(2):
            to = b * 2 + i

            @pl.when(to != me_t)
            def _():
                remote(ctx.at[rows_of(to, 128), :], cr.at[me_t], s_cs, s_cr, (me_r, to)).start()

            @pl.when(to == me_t)
            def _():
                cr[me_t] = ctx[rows_of(to, 128), :]

    for step in range(4):
        gather_sibling(wo, s_wr, step)
    await_bytes(cr.at[pl.ds(0, NTP - 1)], s_cr)
    attended = b_out[...]
    for h in range(NTP):
        attended = attended + dot(cr[h], wo[h])

    def norm(rows, which):
        center = rows - jnp.mean(rows, axis=-1, keepdims=True)
        var = jnp.mean(center * center, axis=-1, keepdims=True)
        return (center * lax.rsqrt(var + 1e-5) * gain[which : which + 1, :] + offset[which : which + 1, :]).astype(BF16)

    nrm[0] = norm(hid[me_t].astype(F32) + attended, 0)

    begin(nrm.at[0, top_half], nrm.at[1, top_half], s_ns.at[0], s_nr.at[0], right)
    begin(nrm.at[0, low_half], nrm.at[2, low_half], s_ns.at[2], s_nr.at[2], left)
    begin(nrm.at[0, low_half], nrm.at[1, low_half], s_ns.at[1], s_nr.at[1], right)
    begin(nrm.at[0, top_half], nrm.at[2, top_half], s_ns.at[3], s_nr.at[3], left)
    await_bytes(w1.at[1 - c], s_er.at[0])
    await_bytes(w2.at[1 - c], s_er.at[1])
    await_bytes(b1.at[1 - c], s_er.at[2])

    def feed(slot):
        rows = nrm[slot]
        total = None
        for i in range(2):
            u = dot(rows, w1[i]) + b1[i]
            u = (0.5 * u * (1.0 + lax.erf(u * 0.7071067811865476))).astype(BF16)
            term = dot(u, w2[i])
            total = term if total is None else total + term
        return total

    own_sum[...] = feed(0)
    await_bytes(nrm.at[1, top_half], s_nr.at[0])
    begin(nrm.at[1, top_half], nrm.at[3, top_half], s_ns.at[4], s_nr.at[4], right)
    await_bytes(nrm.at[2, low_half], s_nr.at[2])
    begin(nrm.at[2, low_half], nrm.at[3, low_half], s_ns.at[5], s_nr.at[5], left)
    await_bytes(nrm.at[1, low_half], s_nr.at[1])
    part[1] = feed(1).astype(BF16)
    begin(part.at[1, top_half], fr.at[top_half], s_fs.at[0], s_fr.at[0], left)
    await_bytes(nrm.at[2, top_half], s_nr.at[3])
    part[2] = feed(2).astype(BF16)
    begin(part.at[2, low_half], fl.at[low_half], s_fs.at[1], s_fr.at[1], right)
    await_bytes(nrm.at[3, top_half], s_nr.at[4])
    await_bytes(nrm.at[3, low_half], s_nr.at[5])
    part[3] = feed(3).astype(BF16)
    begin(part.at[3, top_half], ra, s_fs.at[2], s_fr.at[2], right)
    begin(part.at[3, low_half], rb, s_fs.at[3], s_fr.at[3], left)
    await_bytes(ra, s_fr.at[2])
    part[2, 0:64] = (part[2, 0:64].astype(F32) + ra[...].astype(F32)).astype(BF16)
    begin(part.at[2, top_half], fl.at[top_half], s_fs.at[4], s_fr.at[4], right)
    await_bytes(rb, s_fr.at[3])
    part[1, 64:128] = (part[1, 64:128].astype(F32) + rb[...].astype(F32)).astype(BF16)
    begin(part.at[1, low_half], fr.at[low_half], s_fs.at[5], s_fr.at[5], left)
    await_bytes(fr.at[top_half], s_fr.at[0])
    await_bytes(fl.at[low_half], s_fr.at[1])
    await_bytes(fl.at[top_half], s_fr.at[4])
    await_bytes(fr.at[low_half], s_fr.at[5])
    mixed = own_sum[...] + fl[...].astype(F32) + fr[...].astype(F32) + b_down[...]
    out_ref[...] = norm(nrm[0].astype(F32) + mixed, 1)

    for copy in sent:
        copy.wait_send()
    await_bytes(qa.at[pl.ds(0, NREQ - 1)], s_qas)
    await_bytes(qz.at[pl.ds(1, NZ - 1)], s_qzs)
    for j in range(NLONG):
        await_bytes(pr.at[j, pl.ds(1, NZ - 1)], s_ps.at[j])
    await_bytes(rr.at[pl.ds(0, NREQ - 1)], s_rs)
    await_bytes(cr.at[pl.ds(0, NTP - 1)], s_cs)
    out_copy.wait()


def body(
    hidden_in, short_cache, long_cache, short_len, long_owner, w_qkv, b_qkv, w_out, b_out,
    w_in, b_in, w_down, b_down, norm_gain, norm_offset,
):
    hbm = pl.BlockSpec(memory_space=pl.ANY)
    vmem = pl.BlockSpec(memory_space=pltpu.VMEM)
    smem = pl.BlockSpec(memory_space=pltpu.SMEM)
    V, S = pltpu.VMEM, pltpu.SemaphoreType.DMA
    hidden_out, new_kv = pl.pallas_call(
        kernel,
        out_shape=(
            jax.ShapeDtypeStruct((128, D), BF16),
            jax.ShapeDtypeStruct((2 * SPAN, WIDE), BF16),
        ),
        in_specs=[
            hbm, hbm, hbm, smem, smem, hbm, vmem, hbm, vmem, hbm, hbm, hbm, vmem, vmem, vmem,
        ],
        out_specs=(vmem, hbm),
        scratch_shapes=[
            V((NTP, 128, D), BF16),
            V((D, 3 * WIDE), BF16),
            V((2 * SHORT, WIDE), BF16),
            V((NX, 2 * NLONG * LSEG, WIDE), BF16),
            V((NTP, WIDE, D), BF16),
            V((2, D, FFH), BF16),
            V((2, FFH, D), BF16),
            V((2, 1, FFH), F32),
            V((SPAN, WIDE), BF16),
            V((SHORT + SPAN, WIDE), BF16),
            V((SHORT + SPAN, WIDE), BF16),
            V((NLONG, NX * LSEG, WIDE), BF16),
            V((NLONG, NX * LSEG, WIDE), BF16),
            V((NREQ, CH, WIDE), BF16),
            V((NLONG, CH, WIDE), BF16),
            V((NZ, NLONG, CH, WIDE), BF16),
            V((8, SHORT), F32),
            V((256, 256), BF16),
            V((256, 256), BF16),
            V((4, 2, 256, WIDE), F32),
            V((4, 2, 256, WIDE), F32),
            V((2, 256, WIDE), F32),
            V((2, 256, WIDE), F32),
            V((SPAN, WIDE), F32),
            V((SPAN, WIDE), F32),
            V((SPAN, WIDE), F32),
            V((NLONG, NZ, MSG, WIDE), BF16),
            V((NLONG, NZ, MSG, WIDE), BF16),
            V((NLONG, MSG, WIDE), F32),
            V((NREQ, MSG, WIDE), BF16),
            V((NREQ, MSG, WIDE), BF16),
            V((SPAN, WIDE), BF16),
            V((NTP, 128, WIDE), BF16),
            V((NY, 128, D), BF16),
            V((NY, 128, D), BF16),
            V((128, D), F32),
            V((64, D), BF16),
            V((64, D), BF16),
            V((128, D), BF16),
            V((128, D), BF16),
            V((2 * SPAN, WIDE), BF16),
            S((10,)), S((12,)), S((12,)), S((12,)), S((12,)), S((12,)), S((12,)), S((3,)), S((3,)),
            S, S, S, S, S((3,)), S((3,)), S, S, S, S, S((6,)), S((6,)), S((6,)), S((6,)), S((1,)),
        ],
        compiler_params=pltpu.CompilerParams(
            collective_id=0, has_side_effects=True, vmem_limit_bytes=56 * 1024 * 1024
        ),
    )(
        hidden_in[0],
        short_cache.reshape(2 * SHORT, WIDE),
        long_cache.reshape(2 * NLONG * LSEG, WIDE),
        short_len,
        long_owner,
        w_qkv,
        b_qkv,
        w_out,
        b_out[None],
        w_in,
        b_in[None],
        w_down,
        b_down[None],
        norm_gain,
        norm_offset,
    )
    return (hidden_out[None], new_kv.reshape(1, SPAN, 2, WIDE))


def solution(mesh):
    return jax.shard_map(
        body,
        mesh=mesh,
        in_specs=(
            P("req", "tp", None),
            P("req", None, None, "tp"),
            P(None, "req", None, "tp"),
            P("req"),
            P(),
            P(None, None, "tp"),
            P(None, "tp"),
            P("tp", None),
            P(),
            P(None, "tp"),
            P("tp"),
            P("tp", None),
            P(),
            P(),
            P(),
        ),
        out_specs=(P("req", "tp", None), P("req", None, None, "tp")),
        check_vma=False,
    )
```

```python
import jax
import jax.numpy as jnp
from jax import lax
from jax.experimental import pallas as pl
from jax.experimental.pallas import tpu as pltpu
from jax.sharding import PartitionSpec as P

MESH = pl.DeviceIdType.MESH
F32 = jnp.float32
BF16 = jnp.bfloat16
LOW = -1e30

NREQ, NX, NZ = 32, 4, 8
NTP, NY = 8, 4
SPAN, D, WIDE = 1024, 1024, 128
SHORT, LSEG, NLONG = 1536, 512, 3
CH = 32
FFH = 512
NP = 4


def dot(a, b):
    return jnp.dot(a, b, preferred_element_type=F32)


def dot_t(a, b):
    return lax.dot_general(a, b, (((1,), (1,)), ((), ())), preferred_element_type=F32)


def rows_of(block, size, count=None):
    return pl.ds(pl.multiple_of(block * size, size), count or size)


def kernel(
    hid_hbm, short_hbm, long_hbm, short_len, owner, wqkv_hbm, b_qkv, wout_hbm, b_out,
    win_hbm, bin_hbm, wdown_hbm, b_down, gain, offset,
    out_ref, newkv_hbm,
    hid, wq, short_raw, long_raw, wo, w1, w2, b1, q_s, k_s, v_s, kl, vl, qa, sel, qz, bias,
    spread, weave, m_s, o_s, m_g, o_g, m_l, l_l, o_l, ps, pr, pst, prt, merged, merged_t, rs, rr, rst, rrt, ctx, cr, nrm, part,
    own_sum, ra, rb, fl, fr, kvout,
    s_loc, s_hs, s_hr, s_ws, s_wr, s_xs, s_xr, s_es, s_er, s_qas, s_qar, s_qzs, s_qzr,
    s_ps, s_pr, s_rs, s_rr, s_cs, s_cr, s_ns, s_nr, s_fs, s_fr, s_out,
):
    me_r, me_t = lax.axis_index("req"), lax.axis_index("tp")
    y, c = me_t // 2, me_t % 2
    x, z = me_r // NZ, me_r % NZ
    yl, yr, yf = (y + 3) % 4, (y + 1) % 4, (y + 2) % 4
    right, left = (me_r, yr * 2 + c), (me_r, yl * 2 + c)
    sibling = (me_r, y * 2 + 1 - c)
    right_other, left_other = (me_r, yr * 2 + 1 - c), (me_r, yl * 2 + 1 - c)
    x_right, x_left = (((x + 1) % 4) * NZ + z, me_t), (((x + 3) % 4) * NZ + z, me_t)

    def remote(src, dst, ss, rs_, dev):
        return pltpu.make_async_remote_copy(
            src_ref=src, dst_ref=dst, send_sem=ss, recv_sem=rs_, device_id=dev, device_id_type=MESH
        )

    def await_bytes(ref, sem):
        pltpu.make_async_copy(ref, ref, sem).wait()

    loads = [
        (hid_hbm, hid.at[me_t]),
        (long_hbm, long_raw.at[0]),
        (short_hbm, short_raw),
        (wqkv_hbm.at[0], wq.at[:, pl.ds(0, WIDE)]),
        (wqkv_hbm.at[1], wq.at[:, pl.ds(WIDE, WIDE)]),
        (wqkv_hbm.at[2], wq.at[:, pl.ds(2 * WIDE, WIDE)]),
        (wout_hbm, wo.at[me_t]),
        (win_hbm, w1.at[c]),
        (wdown_hbm, w2.at[c]),
        (bin_hbm, b1.at[c]),
    ]
    loads = [pltpu.make_async_copy(s, d, s_loc.at[i]) for i, (s, d) in enumerate(loads)]
    for load in loads:
        load.start()

    barrier = pltpu.get_barrier_semaphore()

    @pl.loop(1, NREQ)
    def _(d):
        pl.semaphore_signal(barrier, inc=1, device_id=((me_r + d) % NREQ, me_t), device_id_type=MESH)

    @pl.loop(1, NTP)
    def _(d):
        pl.semaphore_signal(barrier, inc=1, device_id=(me_r, (me_t + d) % NTP), device_id_type=MESH)

    pl.semaphore_wait(barrier, NREQ - 1 + NTP - 1)

    top_half, low_half = pl.ds(0, 64), pl.ds(64, 64)

    def begin(*args):
        copy = remote(*args)
        copy.start()
        sent.append(copy)

    def gather_start(buf, ss, sr):
        mine, top, low = buf.at[me_t], buf.at[me_t, top_half], buf.at[me_t, low_half]
        begin(top, top, ss.at[1], sr.at[0], right)
        begin(low, low, ss.at[2], sr.at[2], left)
        begin(top, top, ss.at[10], sr.at[10], right_other)
        begin(low, low, ss.at[11], sr.at[11], left_other)
        begin(low, low, ss.at[3], sr.at[1], right)
        begin(top, top, ss.at[4], sr.at[3], left)
        begin(mine, mine, ss.at[0], sr.at[6], sibling)

    def gather_forward(buf, ss, sr):
        half = buf.at[yl * 2 + c, top_half]
        await_bytes(half, sr.at[0])
        begin(half, half, ss.at[5], sr.at[4], right)
        half = buf.at[yr * 2 + c, low_half]
        await_bytes(half, sr.at[2])
        begin(half, half, ss.at[6], sr.at[5], left)

    def gather_share(buf, ss, sr, step):
        slot = (y, yl, yr, yf)[step] * 2 + c
        if step == 1:
            await_bytes(buf.at[slot, low_half], sr.at[1])
        elif step == 2:
            await_bytes(buf.at[slot, top_half], sr.at[3])
        else:
            await_bytes(buf.at[slot, top_half], sr.at[4])
            await_bytes(buf.at[slot, low_half], sr.at[5])
        share = buf.at[slot] if step == 3 else buf.at[slot, (None, low_half, top_half)[step]]
        begin(share, share, ss.at[6 + step], sr.at[6 + step], sibling)

    def gather_sibling(buf, sr, step):
        slot = (y, yl, yr, yf)[step] * 2 + 1 - c
        if step == 1:
            await_bytes(buf.at[slot, top_half], sr.at[10])
            await_bytes(buf.at[slot, low_half], sr.at[7])
        elif step == 2:
            await_bytes(buf.at[slot, low_half], sr.at[11])
            await_bytes(buf.at[slot, top_half], sr.at[8])
        else:
            await_bytes(buf.at[slot], sr.at[6 + step])

    sent = []
    loads[0].wait()
    gather_start(hid, s_hs, s_hr)
    loads[1].wait()

    def x_rows(j, half=None):
        if half is None:
            return rows_of(j, 2 * LSEG)
        return pl.ds(pl.multiple_of(j * 2 * LSEG + half * LSEG, LSEG), LSEG)

    def x_send(j):
        own = long_raw.at[0, x_rows(j)]
        begin(own, long_raw.at[1, x_rows(j)], s_xs.at[4 * j], s_xr.at[4 * j], x_right)
        begin(own, long_raw.at[2, x_rows(j)], s_xs.at[4 * j + 1], s_xr.at[4 * j + 1], x_left)

    def x_forward(j):
        for half, to in ((0, x_right), (1, x_left)):
            await_bytes(long_raw.at[1 + half, x_rows(j)], s_xr.at[4 * j + half])
            at, k = x_rows(j, half), 4 * j + 2 + half
            begin(long_raw.at[1 + half, at], long_raw.at[3, at], s_xs.at[k], s_xr.at[k], to)

    x_send(0)
    x_send(1)

    row256 = lax.broadcasted_iota(jnp.int32, (256, 256), 0)
    col256 = lax.broadcasted_iota(jnp.int32, (256, 256), 1)
    target = jnp.where(row256 < 128, 2 * row256, 2 * (row256 - 128) + 1)
    spread[...] = jnp.where(col256 == target, 1.0, 0.0).astype(BF16)
    target_t = jnp.where(col256 < 128, 2 * col256, 2 * (col256 - 128) + 1)
    weave[...] = jnp.where(row256 == target_t, 1.0, 0.0).astype(BF16)
    bias[...] = jnp.where(
        lax.broadcasted_iota(jnp.int32, (8, SHORT), 1) < short_len[0], 0.0, LOW
    )
    lane = lax.broadcasted_iota(jnp.int32, (1, WIDE), 1)
    first = jnp.where(lane < 64, 1.0, 0.0).astype(BF16)
    second = jnp.where(lane < 64, 0.0, 1.0).astype(BF16)

    def unweave(tile):
        both = dot(spread[...], tile).astype(BF16)
        return both[:128], both[128:]

    loads[2].wait()

    @pl.loop(0, 3)
    def _(g):
        for i in range(4):
            at = g * 4 + i
            keys, values = unweave(short_raw[rows_of(at, 256), :])
            k_s[rows_of(at, 128), :] = keys
            v_s[rows_of(at, 128), :] = values

    def unweave_long(j, slot):
        for i in range(4):
            keys, values = unweave(long_raw[slot, rows_of(j * 4 + i, 256), :])
            at = pl.ds(slot * LSEG + i * 128, 128)
            kl[j, at, :] = keys
            vl[j, at, :] = values

    for i in (3, 4, 5):
        loads[i].wait()

    def project(t):
        mixed = dot(hid[t], wq[...])
        q = ((mixed[:, :WIDE] + b_qkv[0:1, :]) * 0.125).astype(BF16)
        k = (mixed[:, WIDE : 2 * WIDE] + b_qkv[1:2, :]).astype(BF16)
        v = (mixed[:, 2 * WIDE :] + b_qkv[2:3, :]).astype(BF16)
        q_s[rows_of(t, 128), :] = q
        k_s[pl.ds(pl.multiple_of(SHORT + t * 128, 128), 128), :] = k
        v_s[pl.ds(pl.multiple_of(SHORT + t * 128, 128), 128), :] = v

        @pl.loop(0, 4)
        def _(i):
            to = 4 * t + i

            @pl.when(to != me_r)
            def _():
                remote(q_s.at[rows_of(to, CH), :], qa.at[me_r], s_qas, s_qar, (to, me_t)).start()

            @pl.when(to == me_r)
            def _():
                qa[me_r] = q_s[rows_of(to, CH), :]

    def attend(q, k, v, extra, m_ref, o_ref, fresh):
        vs = (v * first + second, v * second + first)
        scores = [dot_t(q * mask, k) for mask in (first, second)]
        for h, s in enumerate(scores):
            if extra is not None:
                s = extra(s)
            m_new = jnp.max(s, axis=1, keepdims=True)
            if fresh:
                m_new = jnp.broadcast_to(m_new, (256, WIDE))
            else:
                m_old = m_ref[h]
                m_new = jnp.maximum(m_old, m_new)
            wide = jnp.concatenate([m_new] * (s.shape[1] // WIDE), axis=1)
            o = dot(jnp.exp(s - wide).astype(BF16), vs[h])
            o_ref[h] = o if fresh else o_ref[h] * jnp.exp(m_old - m_new) + o
            m_ref[h] = m_new

    def attend_end(m_ref, o_ref):
        low = lax.broadcasted_iota(jnp.int32, (256, WIDE), 1) < 64
        total = pltpu.roll(jnp.where(low, o_ref[1], o_ref[0]), 64, 1)
        return jnp.where(low, m_ref[0], m_ref[1]), total, jnp.where(low, o_ref[0], o_ref[1])

    m_s[...] = jnp.full(m_s.shape, LOW, F32)
    o_s[...] = jnp.zeros(o_s.shape, F32)

    def attend_short(b):
        attend(
            q_s[rows_of(b, 256), :], k_s[:SHORT, :], v_s[:SHORT, :], lambda s: s + bias[0:1, :],
            m_s.at[b], o_s.at[b], False,
        )

    def attend_new(b):
        at = slice(SHORT, SHORT + 256 * (b + 1))
        causal = jnp.where(col256 <= row256, 0.0, LOW)

        def extra(s):
            last = s[:, 256 * b :] + causal
            return jnp.concatenate([s[:, : 256 * b], last], axis=1) if b else last

        attend(q_s[b * 256 : (b + 1) * 256, :], k_s[at, :], v_s[at, :], extra, m_s.at[b], o_s.at[b], False)

    def attend_local_end(b):
        m, total, o = attend_end(m_s.at[b], o_s.at[b])
        m_l[rows_of(b, 256), :] = m
        l_l[rows_of(b, 256), :] = total
        o_l[rows_of(b, 256), :] = o

    project(me_t)
    gather_sibling(hid, s_hr, 0)
    project(y * 2 + 1 - c)
    attend_short(y)
    gather_forward(hid, s_hs, s_hr)
    gather_share(hid, s_hs, s_hr, 1)
    project(yl * 2 + c)
    gather_share(hid, s_hs, s_hr, 2)
    project(yr * 2 + c)
    gather_sibling(hid, s_hr, 1)
    project(yl * 2 + 1 - c)
    x_forward(0)
    gather_share(hid, s_hs, s_hr, 3)
    project(yf * 2 + c)
    gather_sibling(hid, s_hr, 2)
    project(yr * 2 + 1 - c)
    gather_sibling(hid, s_hr, 3)
    project(yf * 2 + 1 - c)

    for i in (6, 7, 8, 9):
        loads[i].wait()
    gather_start(wo, s_ws, s_wr)
    begin(w1.at[c], w1.at[c], s_es.at[0], s_er.at[0], sibling)
    begin(w2.at[c], w2.at[c], s_es.at[1], s_er.at[1], sibling)
    begin(b1.at[c], b1.at[c], s_es.at[2], s_er.at[2], sibling)
    x_forward(1)
    for j in range(NLONG):
        unweave_long(j, 0)
    attend_short(yl)

    lane32 = lax.broadcasted_iota(jnp.int32, (CH, WIDE), 1) % 64
    diagonal = jnp.where(lane32 == lax.broadcasted_iota(jnp.int32, (CH, WIDE), 0), 1.0, 0.0)
    side_r = lax.broadcasted_iota(jnp.int32, (WIDE, WIDE), 0) // 64
    side_c = lax.broadcasted_iota(jnp.int32, (WIDE, WIDE), 1) // 64
    sides = jnp.where(side_r == side_c, 1.0, 0.0).astype(BF16)

    def pack_stats(lse):
        return jnp.sum(lse * diagonal, axis=0, keepdims=True)

    def unpack_stats(rows):
        n, rest, lse = rows.shape[0], rows, None
        for _ in range(3):
            piece = rest.astype(BF16).astype(F32)
            rest = rest - piece
            term = dot((piece * diagonal[None]).reshape(n * CH, WIDE).astype(BF16), sides)
            lse = term if lse is None else lse + term
        return lse

    await_bytes(qa.at[pl.ds(0, NREQ - 1)], s_qar)
    for j in range(NLONG):
        sel[j] = qa[owner[j]]
    qz[0] = sel[...]

    @pl.loop(1, NZ)
    def _(d):
        to = x * NZ + (z + d) % NZ
        remote(sel, qz.at[d], s_qzs, s_qzr, (to, me_t)).start()

    x_send(2)

    @pl.loop(0, 4)
    def _(g):
        for i in range(2):
            t = g * 2 + i
            at = pl.ds(pl.multiple_of(SHORT + t * 128, 128), 128)
            both = jnp.concatenate([k_s[at, :], v_s[at, :]], axis=0)
            kvout[rows_of(t, 256), :] = dot(weave[...], both).astype(BF16)

    out_copy = pltpu.make_async_copy(kvout, newkv_hbm, s_out.at[0])
    out_copy.start()
    gather_forward(wo, s_ws, s_wr)
    attend_new(0)
    attend_new(1)
    for j in range(2):
        unweave_long(j, 1)
        unweave_long(j, 2)
    x_forward(2)
    unweave_long(2, 1)
    unweave_long(2, 2)
    for step in (1, 2, 3):
        gather_share(wo, s_ws, s_wr, step)
    await_bytes(qz.at[pl.ds(1, NZ - 1)], s_qzr)

    @pl.loop(0, NLONG)
    def _(j):
        for half in range(2):
            await_bytes(long_raw.at[3, x_rows(j, half)], s_xr.at[4 * j + 2 + half])
        unweave_long(j, 3)
        attend(qz[:, j].reshape(256, WIDE), kl[j], vl[j], None, m_g, o_g, True)
        m, total, o = attend_end(m_g, o_g)
        lse = m + jnp.log(total)
        o = (o / total).astype(BF16)
        for d in range(NZ):
            at = slice(d * CH, (d + 1) * CH)
            dst, dst_stats = (pr, prt) if d == 0 else (ps, pst)
            dst[j, d] = o[at]
            dst_stats[j, d] = pack_stats(lse[at])

        @pl.loop(1, NZ)
        def _(d):
            to = (x * NZ + (z + NZ - d) % NZ, me_t)
            remote(ps.at[j, d], pr.at[j, d], s_ps.at[j], s_pr.at[j], to).start()
            remote(pst.at[j, d], prt.at[j, d], s_ps.at[3 + j], s_pr.at[3 + j], to).start()

    attend_short(yr)
    attend_new(2)

    @pl.loop(0, NLONG)
    def _(j):
        await_bytes(pr.at[j, pl.ds(1, NZ - 1)], s_pr.at[j])
        await_bytes(prt.at[j, pl.ds(1, NZ - 1)], s_pr.at[3 + j])
        lse = unpack_stats(prt[j]).reshape(NZ, CH, WIDE)
        top = jnp.max(lse, axis=0, keepdims=True)
        w = jnp.exp(lse - top)
        total = jnp.sum(w, axis=0)
        merged[j] = jnp.sum(w * pr[j].astype(F32), axis=0) / total
        merged_t[j] = pack_stats(top[0] + jnp.log(total))

    @pl.loop(0, NREQ)
    def _(r):
        value, stats, rest = None, None, 1.0
        for j in range(NLONG):
            mine = jnp.where(owner[j] == r, 1.0, 0.0)
            value = merged[j] * mine if j == 0 else value + merged[j] * mine
            stats = merged_t[j] * mine if j == 0 else stats + merged_t[j] * mine
            rest = rest - mine
        value, stats = value.astype(BF16), stats + LOW * rest

        @pl.when(r == me_r)
        def _():
            rr[me_r] = value
            rrt[me_r] = stats

        @pl.when(r != me_r)
        def _():
            rs[r] = value
            rst[r] = stats
            remote(rs.at[r], rr.at[me_r], s_rs.at[0], s_rr.at[0], (r, me_t)).start()
            remote(rst.at[r], rrt.at[me_r], s_rs.at[1], s_rr.at[1], (r, me_t)).start()

    attend_short(yf)
    attend_new(3)
    for b in range(4):
        attend_local_end(b)

    await_bytes(rr.at[pl.ds(0, NREQ - 1)], s_rr.at[0])
    await_bytes(rrt.at[pl.ds(0, NREQ - 1)], s_rr.at[1])

    @pl.loop(0, 4)
    def _(b):
        at = rows_of(b, 256)
        lse = unpack_stats(rrt[pl.ds(b * 8, 8)])
        o = rr[pl.ds(b * 8, 8)].astype(F32).reshape(256, WIDE)
        m = m_l[at, :]
        top = jnp.maximum(m, lse)
        a, w = jnp.exp(m - top), jnp.exp(lse - top)
        value = (o_l[at, :] * a + o * w) / (l_l[at, :] * a + w)
        ctx[at, :] = value.astype(BF16)
        for i in range(2):
            to = b * 2 + i

            @pl.when(to != me_t)
            def _():
                remote(ctx.at[rows_of(to, 128), :], cr.at[me_t], s_cs, s_cr, (me_r, to)).start()

            @pl.when(to == me_t)
            def _():
                cr[me_t] = ctx[rows_of(to, 128), :]

    for step in range(4):
        gather_sibling(wo, s_wr, step)
    await_bytes(cr.at[pl.ds(0, NTP - 1)], s_cr)
    attended = b_out[...]
    for h in range(NTP):
        attended = attended + dot(cr[h], wo[h])

    def norm(rows, which):
        center = rows - jnp.mean(rows, axis=-1, keepdims=True)
        var = jnp.mean(center * center, axis=-1, keepdims=True)
        return (center * lax.rsqrt(var + 1e-5) * gain[which : which + 1, :] + offset[which : which + 1, :]).astype(BF16)

    nrm[0] = norm(hid[me_t].astype(F32) + attended, 0)

    begin(nrm.at[0, top_half], nrm.at[1, top_half], s_ns.at[0], s_nr.at[0], right)
    begin(nrm.at[0, low_half], nrm.at[2, low_half], s_ns.at[2], s_nr.at[2], left)
    begin(nrm.at[0, low_half], nrm.at[1, low_half], s_ns.at[1], s_nr.at[1], right)
    begin(nrm.at[0, top_half], nrm.at[2, top_half], s_ns.at[3], s_nr.at[3], left)
    await_bytes(w1.at[1 - c], s_er.at[0])
    await_bytes(w2.at[1 - c], s_er.at[1])
    await_bytes(b1.at[1 - c], s_er.at[2])

    def feed(slot):
        rows = nrm[slot]
        total = None
        for i in range(2):
            u = dot(rows, w1[i]) + b1[i]
            u = (0.5 * u * (1.0 + lax.erf(u * 0.7071067811865476))).astype(BF16)
            term = dot(u, w2[i])
            total = term if total is None else total + term
        return total

    def piece(i):
        return pl.ds(i * (D // NP), D // NP)

    own_sum[...] = feed(0)
    await_bytes(nrm.at[1, top_half], s_nr.at[0])
    begin(nrm.at[1, top_half], nrm.at[3, top_half], s_ns.at[4], s_nr.at[4], right)
    await_bytes(nrm.at[2, low_half], s_nr.at[2])
    begin(nrm.at[2, low_half], nrm.at[3, low_half], s_ns.at[5], s_nr.at[5], left)
    await_bytes(nrm.at[1, low_half], s_nr.at[1])
    part[1] = feed(1).astype(BF16)
    begin(part.at[1, top_half], fr.at[top_half], s_fs.at[0], s_fr.at[0], left)
    await_bytes(nrm.at[2, top_half], s_nr.at[3])
    part[2] = feed(2).astype(BF16)
    begin(part.at[2, low_half], fl.at[low_half], s_fs.at[1], s_fr.at[1], right)
    await_bytes(nrm.at[3, top_half], s_nr.at[4])
    await_bytes(nrm.at[3, low_half], s_nr.at[5])
    part[3] = feed(3).astype(BF16)
    for i in range(NP):
        begin(part.at[3, top_half, piece(i)], ra.at[:, piece(i)], s_fs.at[2 + 4 * i], s_fr.at[2 + 4 * i], right)
        begin(part.at[3, low_half, piece(i)], rb.at[:, piece(i)], s_fs.at[3 + 4 * i], s_fr.at[3 + 4 * i], left)
    for i in range(NP):
        at = piece(i)
        await_bytes(ra.at[:, at], s_fr.at[2 + 4 * i])
        part[2, 0:64, at] = (part[2, 0:64, at].astype(F32) + ra[:, at].astype(F32)).astype(BF16)
        begin(part.at[2, top_half, at], fl.at[top_half, at], s_fs.at[4 + 4 * i], s_fr.at[4 + 4 * i], right)
        await_bytes(rb.at[:, at], s_fr.at[3 + 4 * i])
        part[1, 64:128, at] = (part[1, 64:128, at].astype(F32) + rb[:, at].astype(F32)).astype(BF16)
        begin(part.at[1, low_half, at], fr.at[low_half, at], s_fs.at[5 + 4 * i], s_fr.at[5 + 4 * i], left)
    await_bytes(fr.at[top_half], s_fr.at[0])
    await_bytes(fl.at[low_half], s_fr.at[1])
    for i in range(NP):
        await_bytes(fl.at[top_half, piece(i)], s_fr.at[4 + 4 * i])
        await_bytes(fr.at[low_half, piece(i)], s_fr.at[5 + 4 * i])
    mixed = own_sum[...] + fl[...].astype(F32) + fr[...].astype(F32) + b_down[...]
    out_ref[...] = norm(nrm[0].astype(F32) + mixed, 1)

    for copy in sent:
        copy.wait_send()
    await_bytes(qa.at[pl.ds(0, NREQ - 1)], s_qas)
    await_bytes(qz.at[pl.ds(1, NZ - 1)], s_qzs)
    for j in range(NLONG):
        await_bytes(pr.at[j, pl.ds(1, NZ - 1)], s_ps.at[j])
        await_bytes(prt.at[j, pl.ds(1, NZ - 1)], s_ps.at[3 + j])
    await_bytes(rr.at[pl.ds(0, NREQ - 1)], s_rs.at[0])
    await_bytes(rrt.at[pl.ds(0, NREQ - 1)], s_rs.at[1])
    await_bytes(cr.at[pl.ds(0, NTP - 1)], s_cs)
    out_copy.wait()


def body(
    hidden_in, short_cache, long_cache, short_len, long_owner, w_qkv, b_qkv, w_out, b_out,
    w_in, b_in, w_down, b_down, norm_gain, norm_offset,
):
    hbm = pl.BlockSpec(memory_space=pl.ANY)
    vmem = pl.BlockSpec(memory_space=pltpu.VMEM)
    smem = pl.BlockSpec(memory_space=pltpu.SMEM)
    V, S = pltpu.VMEM, pltpu.SemaphoreType.DMA
    hidden_out, new_kv = pl.pallas_call(
        kernel,
        out_shape=(
            jax.ShapeDtypeStruct((128, D), BF16),
            jax.ShapeDtypeStruct((2 * SPAN, WIDE), BF16),
        ),
        in_specs=[
            hbm, hbm, hbm, smem, smem, hbm, vmem, hbm, vmem, hbm, hbm, hbm, vmem, vmem, vmem,
        ],
        out_specs=(vmem, hbm),
        scratch_shapes=[
            V((NTP, 128, D), BF16),
            V((D, 3 * WIDE), BF16),
            V((2 * SHORT, WIDE), BF16),
            V((NX, 2 * NLONG * LSEG, WIDE), BF16),
            V((NTP, WIDE, D), BF16),
            V((2, D, FFH), BF16),
            V((2, FFH, D), BF16),
            V((2, 1, FFH), F32),
            V((SPAN, WIDE), BF16),
            V((SHORT + SPAN, WIDE), BF16),
            V((SHORT + SPAN, WIDE), BF16),
            V((NLONG, NX * LSEG, WIDE), BF16),
            V((NLONG, NX * LSEG, WIDE), BF16),
            V((NREQ, CH, WIDE), BF16),
            V((NLONG, CH, WIDE), BF16),
            V((NZ, NLONG, CH, WIDE), BF16),
            V((8, SHORT), F32),
            V((256, 256), BF16),
            V((256, 256), BF16),
            V((4, 2, 256, WIDE), F32),
            V((4, 2, 256, WIDE), F32),
            V((2, 256, WIDE), F32),
            V((2, 256, WIDE), F32),
            V((SPAN, WIDE), F32),
            V((SPAN, WIDE), F32),
            V((SPAN, WIDE), F32),
            V((NLONG, NZ, CH, WIDE), BF16),
            V((NLONG, NZ, CH, WIDE), BF16),
            V((NLONG, NZ, 1, WIDE), F32),
            V((NLONG, NZ, 1, WIDE), F32),
            V((NLONG, CH, WIDE), F32),
            V((NLONG, 1, WIDE), F32),
            V((NREQ, CH, WIDE), BF16),
            V((NREQ, CH, WIDE), BF16),
            V((NREQ, 1, WIDE), F32),
            V((NREQ, 1, WIDE), F32),
            V((SPAN, WIDE), BF16),
            V((NTP, 128, WIDE), BF16),
            V((NY, 128, D), BF16),
            V((NY, 128, D), BF16),
            V((128, D), F32),
            V((64, D), BF16),
            V((64, D), BF16),
            V((128, D), BF16),
            V((128, D), BF16),
            V((2 * SPAN, WIDE), BF16),
            S((10,)), S((12,)), S((12,)), S((12,)), S((12,)), S((12,)), S((12,)), S((3,)), S((3,)),
            S, S, S, S, S((6,)), S((6,)), S((2,)), S((2,)), S, S, S((6,)), S((6,)),
            S((2 + 4 * NP,)), S((2 + 4 * NP,)), S((1,)),
        ],
        compiler_params=pltpu.CompilerParams(
            collective_id=0, has_side_effects=True, vmem_limit_bytes=56 * 1024 * 1024
        ),
    )(
        hidden_in[0],
        short_cache.reshape(2 * SHORT, WIDE),
        long_cache.reshape(2 * NLONG * LSEG, WIDE),
        short_len,
        long_owner,
        w_qkv,
        b_qkv,
        w_out,
        b_out[None],
        w_in,
        b_in[None],
        w_down,
        b_down[None],
        norm_gain,
        norm_offset,
    )
    return (hidden_out[None], new_kv.reshape(1, SPAN, 2, WIDE))


def solution(mesh):
    return jax.shard_map(
        body,
        mesh=mesh,
        in_specs=(
            P("req", "tp", None),
            P("req", None, None, "tp"),
            P(None, "req", None, "tp"),
            P("req"),
            P(),
            P(None, None, "tp"),
            P(None, "tp"),
            P("tp", None),
            P(),
            P(None, "tp"),
            P("tp"),
            P("tp", None),
            P(),
            P(),
            P(),
        ),
        out_specs=(P("req", "tp", None), P("req", None, None, "tp")),
        check_vma=False,
    )
```

```python
import jax
import jax.numpy as jnp
from jax import lax
from jax.experimental import pallas as pl
from jax.experimental.pallas import tpu as pltpu
from jax.sharding import PartitionSpec as P

MESH = pl.DeviceIdType.MESH
F32 = jnp.float32
BF16 = jnp.bfloat16
LOW = -1e30

NREQ, NX, NZ = 32, 4, 8
NTP, NY = 8, 4
SPAN, D, WIDE = 1024, 1024, 128
SHORT, LSEG, NLONG = 1536, 512, 3
CH = 32
FFH = 512
NP = 4


def dot(a, b):
    return jnp.dot(a, b, preferred_element_type=F32)


def dot_t(a, b):
    return lax.dot_general(a, b, (((1,), (1,)), ((), ())), preferred_element_type=F32)


def rows_of(block, size, count=None):
    return pl.ds(pl.multiple_of(block * size, size), count or size)


def kernel(
    hid_hbm, short_hbm, long_hbm, short_len, owner, wqkv_hbm, b_qkv, wout_hbm, b_out,
    win_hbm, bin_hbm, wdown_hbm, b_down, gain, offset,
    out_ref, newkv_hbm,
    hid, wq, short_raw, long_raw, wo, w1, w2, b1, q_s, k_s, v_s, kl, vl, qa, sel, qz, bias,
    spread, weave, m_s, o_s, m_g, o_g, m_l, l_l, o_l, ps, pr, pst, prt, merged, merged_t, rs, rr, rst, rrt, ctx, cr, nrm, part,
    own_sum, ra, rb, fl, fr, kvout,
    s_loc, s_hs, s_hr, s_ws, s_wr, s_xs, s_xr, s_es, s_er, s_qas, s_qar, s_qzs, s_qzr,
    s_ps, s_pr, s_rs, s_rr, s_cs, s_cr, s_ns, s_nr, s_fs, s_fr, s_out,
):
    me_r, me_t = lax.axis_index("req"), lax.axis_index("tp")
    y, c = me_t // 2, me_t % 2
    x, z = me_r // NZ, me_r % NZ
    yl, yr, yf = (y + 3) % 4, (y + 1) % 4, (y + 2) % 4
    right, left = (me_r, yr * 2 + c), (me_r, yl * 2 + c)
    sibling = (me_r, y * 2 + 1 - c)
    right_other, left_other = (me_r, yr * 2 + 1 - c), (me_r, yl * 2 + 1 - c)
    x_right, x_left = (((x + 1) % 4) * NZ + z, me_t), (((x + 3) % 4) * NZ + z, me_t)

    def remote(src, dst, ss, rs_, dev):
        return pltpu.make_async_remote_copy(
            src_ref=src, dst_ref=dst, send_sem=ss, recv_sem=rs_, device_id=dev, device_id_type=MESH
        )

    def await_bytes(ref, sem):
        pltpu.make_async_copy(ref, ref, sem).wait()

    loads = [
        (hid_hbm, hid.at[me_t]),
        (long_hbm, long_raw.at[0]),
        (short_hbm, short_raw),
        (wqkv_hbm.at[0], wq.at[:, pl.ds(0, WIDE)]),
        (wqkv_hbm.at[1], wq.at[:, pl.ds(WIDE, WIDE)]),
        (wqkv_hbm.at[2], wq.at[:, pl.ds(2 * WIDE, WIDE)]),
        (wout_hbm, wo.at[me_t]),
        (win_hbm, w1.at[c]),
        (wdown_hbm, w2.at[c]),
        (bin_hbm, b1.at[c]),
    ]
    loads = [pltpu.make_async_copy(s, d, s_loc.at[i]) for i, (s, d) in enumerate(loads)]
    for load in loads:
        load.start()

    barrier = pltpu.get_barrier_semaphore()

    @pl.loop(1, NREQ)
    def _(d):
        pl.semaphore_signal(barrier, inc=1, device_id=((me_r + d) % NREQ, me_t), device_id_type=MESH)

    @pl.loop(1, NTP)
    def _(d):
        pl.semaphore_signal(barrier, inc=1, device_id=(me_r, (me_t + d) % NTP), device_id_type=MESH)

    pl.semaphore_wait(barrier, NREQ - 1 + NTP - 1)

    top_half, low_half = pl.ds(0, 64), pl.ds(64, 64)

    def begin(*args):
        copy = remote(*args)
        copy.start()
        sent.append(copy)

    def gather_start(buf, ss, sr):
        mine, top, low = buf.at[me_t], buf.at[me_t, top_half], buf.at[me_t, low_half]
        begin(top, top, ss.at[1], sr.at[0], right)
        begin(low, low, ss.at[2], sr.at[2], left)
        begin(top, top, ss.at[10], sr.at[10], right_other)
        begin(low, low, ss.at[11], sr.at[11], left_other)
        begin(low, low, ss.at[3], sr.at[1], right)
        begin(top, top, ss.at[4], sr.at[3], left)
        begin(mine, mine, ss.at[0], sr.at[6], sibling)

    def gather_forward(buf, ss, sr):
        half = buf.at[yl * 2 + c, top_half]
        await_bytes(half, sr.at[0])
        begin(half, half, ss.at[5], sr.at[4], right)
        half = buf.at[yr * 2 + c, low_half]
        await_bytes(half, sr.at[2])
        begin(half, half, ss.at[6], sr.at[5], left)

    def gather_share(buf, ss, sr, step):
        slot = (y, yl, yr, yf)[step] * 2 + c
        if step == 1:
            await_bytes(buf.at[slot, low_half], sr.at[1])
        elif step == 2:
            await_bytes(buf.at[slot, top_half], sr.at[3])
        else:
            await_bytes(buf.at[slot, top_half], sr.at[4])
            await_bytes(buf.at[slot, low_half], sr.at[5])
        share = buf.at[slot] if step == 3 else buf.at[slot, (None, low_half, top_half)[step]]
        begin(share, share, ss.at[6 + step], sr.at[6 + step], sibling)

    def gather_sibling(buf, sr, step):
        slot = (y, yl, yr, yf)[step] * 2 + 1 - c
        if step == 1:
            await_bytes(buf.at[slot, top_half], sr.at[10])
            await_bytes(buf.at[slot, low_half], sr.at[7])
        elif step == 2:
            await_bytes(buf.at[slot, low_half], sr.at[11])
            await_bytes(buf.at[slot, top_half], sr.at[8])
        else:
            await_bytes(buf.at[slot], sr.at[6 + step])

    sent = []
    loads[0].wait()
    gather_start(hid, s_hs, s_hr)
    loads[1].wait()

    def x_rows(j, half=None):
        if half is None:
            return rows_of(j, 2 * LSEG)
        return pl.ds(pl.multiple_of(j * 2 * LSEG + half * LSEG, LSEG), LSEG)

    def x_send(j):
        own = long_raw.at[0, x_rows(j)]
        begin(own, long_raw.at[1, x_rows(j)], s_xs.at[4 * j], s_xr.at[4 * j], x_right)
        begin(own, long_raw.at[2, x_rows(j)], s_xs.at[4 * j + 1], s_xr.at[4 * j + 1], x_left)

    def x_forward(j):
        for half, to in ((0, x_right), (1, x_left)):
            await_bytes(long_raw.at[1 + half, x_rows(j)], s_xr.at[4 * j + half])
            at, k = x_rows(j, half), 4 * j + 2 + half
            begin(long_raw.at[1 + half, at], long_raw.at[3, at], s_xs.at[k], s_xr.at[k], to)

    x_send(0)
    x_send(1)

    row256 = lax.broadcasted_iota(jnp.int32, (256, 256), 0)
    col256 = lax.broadcasted_iota(jnp.int32, (256, 256), 1)
    target = jnp.where(row256 < 128, 2 * row256, 2 * (row256 - 128) + 1)
    spread[...] = jnp.where(col256 == target, 1.0, 0.0).astype(BF16)
    target_t = jnp.where(col256 < 128, 2 * col256, 2 * (col256 - 128) + 1)
    weave[...] = jnp.where(row256 == target_t, 1.0, 0.0).astype(BF16)
    bias[...] = jnp.where(
        lax.broadcasted_iota(jnp.int32, (8, SHORT), 1) < short_len[0], 0.0, LOW
    )
    lane = lax.broadcasted_iota(jnp.int32, (1, WIDE), 1)
    first = jnp.where(lane < 64, 1.0, 0.0).astype(BF16)
    second = jnp.where(lane < 64, 0.0, 1.0).astype(BF16)

    def unweave(tile):
        both = dot(spread[...], tile).astype(BF16)
        return both[:128], both[128:]

    loads[2].wait()

    @pl.loop(0, 3)
    def _(g):
        for i in range(4):
            at = g * 4 + i
            keys, values = unweave(short_raw[rows_of(at, 256), :])
            k_s[rows_of(at, 128), :] = keys
            v_s[rows_of(at, 128), :] = values

    def unweave_long(j, slot):
        for i in range(4):
            keys, values = unweave(long_raw[slot, rows_of(j * 4 + i, 256), :])
            at = pl.ds(slot * LSEG + i * 128, 128)
            kl[j, at, :] = keys
            vl[j, at, :] = values

    for i in (3, 4, 5):
        loads[i].wait()

    def project(t):
        mixed = dot(hid[t], wq[...])
        q = ((mixed[:, :WIDE] + b_qkv[0:1, :]) * 0.125).astype(BF16)
        k = (mixed[:, WIDE : 2 * WIDE] + b_qkv[1:2, :]).astype(BF16)
        v = (mixed[:, 2 * WIDE :] + b_qkv[2:3, :]).astype(BF16)
        q_s[rows_of(t, 128), :] = q
        k_s[pl.ds(pl.multiple_of(SHORT + t * 128, 128), 128), :] = k
        v_s[pl.ds(pl.multiple_of(SHORT + t * 128, 128), 128), :] = v

        @pl.loop(0, 4)
        def _(i):
            to, at = i * NZ + t, rows_of(4 * t + i, CH)

            @pl.when(to != me_r)
            def _():
                remote(q_s.at[at, :], qa.at[me_r], s_qas, s_qar, (to, me_t)).start()

            @pl.when(to == me_r)
            def _():
                qa[me_r] = q_s[at, :]

    def attend(q, k, v, extra, m_ref, o_ref, fresh):
        vs = (v * first + second, v * second + first)
        scores = [dot_t(q * mask, k) for mask in (first, second)]
        for h, s in enumerate(scores):
            if extra is not None:
                s = extra(s)
            m_new = jnp.max(s, axis=1, keepdims=True)
            if fresh:
                m_new = jnp.broadcast_to(m_new, (256, WIDE))
            else:
                m_old = m_ref[h]
                m_new = jnp.maximum(m_old, m_new)
            wide = jnp.concatenate([m_new] * (s.shape[1] // WIDE), axis=1)
            o = dot(jnp.exp(s - wide).astype(BF16), vs[h])
            o_ref[h] = o if fresh else o_ref[h] * jnp.exp(m_old - m_new) + o
            m_ref[h] = m_new

    def attend_end(m_ref, o_ref):
        low = lax.broadcasted_iota(jnp.int32, (256, WIDE), 1) < 64
        total = pltpu.roll(jnp.where(low, o_ref[1], o_ref[0]), 64, 1)
        return jnp.where(low, m_ref[0], m_ref[1]), total, jnp.where(low, o_ref[0], o_ref[1])

    m_s[...] = jnp.full(m_s.shape, LOW, F32)
    o_s[...] = jnp.zeros(o_s.shape, F32)

    def attend_short(b):
        attend(
            q_s[rows_of(b, 256), :], k_s[:SHORT, :], v_s[:SHORT, :], lambda s: s + bias[0:1, :],
            m_s.at[b], o_s.at[b], False,
        )

    def attend_new(b):
        at = slice(SHORT, SHORT + 256 * (b + 1))
        causal = jnp.where(col256 <= row256, 0.0, LOW)

        def extra(s):
            last = s[:, 256 * b :] + causal
            return jnp.concatenate([s[:, : 256 * b], last], axis=1) if b else last

        attend(q_s[b * 256 : (b + 1) * 256, :], k_s[at, :], v_s[at, :], extra, m_s.at[b], o_s.at[b], False)

    def attend_local_end(b):
        m, total, o = attend_end(m_s.at[b], o_s.at[b])
        m_l[rows_of(b, 256), :] = m
        l_l[rows_of(b, 256), :] = total
        o_l[rows_of(b, 256), :] = o

    project(me_t)
    gather_sibling(hid, s_hr, 0)
    project(y * 2 + 1 - c)
    attend_short(y)
    gather_forward(hid, s_hs, s_hr)
    gather_share(hid, s_hs, s_hr, 1)
    project(yl * 2 + c)
    gather_share(hid, s_hs, s_hr, 2)
    project(yr * 2 + c)
    gather_sibling(hid, s_hr, 1)
    project(yl * 2 + 1 - c)
    x_forward(0)
    gather_share(hid, s_hs, s_hr, 3)
    project(yf * 2 + c)
    gather_sibling(hid, s_hr, 2)
    project(yr * 2 + 1 - c)
    gather_sibling(hid, s_hr, 3)
    project(yf * 2 + 1 - c)

    for i in (6, 7, 8, 9):
        loads[i].wait()
    gather_start(wo, s_ws, s_wr)
    begin(w1.at[c], w1.at[c], s_es.at[0], s_er.at[0], sibling)
    begin(w2.at[c], w2.at[c], s_es.at[1], s_er.at[1], sibling)
    begin(b1.at[c], b1.at[c], s_es.at[2], s_er.at[2], sibling)
    x_forward(1)
    for j in range(NLONG):
        unweave_long(j, 0)
    attend_short(yl)

    lane32 = lax.broadcasted_iota(jnp.int32, (CH, WIDE), 1) % 64
    diagonal = jnp.where(lane32 == lax.broadcasted_iota(jnp.int32, (CH, WIDE), 0), 1.0, 0.0)
    side_r = lax.broadcasted_iota(jnp.int32, (WIDE, WIDE), 0) // 64
    side_c = lax.broadcasted_iota(jnp.int32, (WIDE, WIDE), 1) // 64
    sides = jnp.where(side_r == side_c, 1.0, 0.0).astype(BF16)

    def pack_stats(lse):
        return jnp.sum(lse * diagonal, axis=0, keepdims=True)

    def unpack_stats(rows):
        n, rest, lse = rows.shape[0], rows, None
        for _ in range(3):
            piece = rest.astype(BF16).astype(F32)
            rest = rest - piece
            term = dot((piece * diagonal[None]).reshape(n * CH, WIDE).astype(BF16), sides)
            lse = term if lse is None else lse + term
        return lse

    await_bytes(qa.at[pl.ds(0, NREQ - 1)], s_qar)
    for j in range(NLONG):
        sel[j] = qa[owner[j]]
    qz[0] = sel[...]

    @pl.loop(1, NZ)
    def _(d):
        to = x * NZ + (z + d) % NZ
        remote(sel, qz.at[d], s_qzs, s_qzr, (to, me_t)).start()

    x_send(2)

    @pl.loop(0, 4)
    def _(g):
        for i in range(2):
            t = g * 2 + i
            at = pl.ds(pl.multiple_of(SHORT + t * 128, 128), 128)
            both = jnp.concatenate([k_s[at, :], v_s[at, :]], axis=0)
            kvout[rows_of(t, 256), :] = dot(weave[...], both).astype(BF16)

    out_copy = pltpu.make_async_copy(kvout, newkv_hbm, s_out.at[0])
    out_copy.start()
    gather_forward(wo, s_ws, s_wr)
    attend_new(0)
    attend_new(1)
    for j in range(2):
        unweave_long(j, 1)
        unweave_long(j, 2)
    x_forward(2)
    unweave_long(2, 1)
    unweave_long(2, 2)
    for step in (1, 2, 3):
        gather_share(wo, s_ws, s_wr, step)
    await_bytes(qz.at[pl.ds(1, NZ - 1)], s_qzr)

    @pl.loop(0, NLONG)
    def _(j):
        for half in range(2):
            await_bytes(long_raw.at[3, x_rows(j, half)], s_xr.at[4 * j + 2 + half])
        unweave_long(j, 3)
        attend(qz[:, j].reshape(256, WIDE), kl[j], vl[j], None, m_g, o_g, True)
        m, total, o = attend_end(m_g, o_g)
        lse = m + jnp.log(total)
        o = (o / total).astype(BF16)
        for d in range(NZ):
            at = slice(d * CH, (d + 1) * CH)
            dst, dst_stats = (pr, prt) if d == 0 else (ps, pst)
            dst[j, d] = o[at]
            dst_stats[j, d] = pack_stats(lse[at])

        @pl.loop(1, NZ)
        def _(d):
            to = (x * NZ + (z + NZ - d) % NZ, me_t)
            remote(ps.at[j, d], pr.at[j, d], s_ps.at[j], s_pr.at[j], to).start()
            remote(pst.at[j, d], prt.at[j, d], s_ps.at[3 + j], s_pr.at[3 + j], to).start()

    attend_short(yr)
    attend_new(2)

    @pl.loop(0, NLONG)
    def _(j):
        await_bytes(pr.at[j, pl.ds(1, NZ - 1)], s_pr.at[j])
        await_bytes(prt.at[j, pl.ds(1, NZ - 1)], s_pr.at[3 + j])
        lse = unpack_stats(prt[j]).reshape(NZ, CH, WIDE)
        top = jnp.max(lse, axis=0, keepdims=True)
        w = jnp.exp(lse - top)
        total = jnp.sum(w, axis=0)
        merged[j] = jnp.sum(w * pr[j].astype(F32), axis=0) / total
        merged_t[j] = pack_stats(top[0] + jnp.log(total))

    chunk = z * NX + x

    @pl.loop(0, NREQ)
    def _(d):
        r = (me_r + 1 + d) % NREQ
        value, stats, rest = None, None, 1.0
        for j in range(NLONG):
            mine = jnp.where(owner[j] == r, 1.0, 0.0)
            value = merged[j] * mine if j == 0 else value + merged[j] * mine
            stats = merged_t[j] * mine if j == 0 else stats + merged_t[j] * mine
            rest = rest - mine
        value, stats = value.astype(BF16), stats + LOW * rest

        @pl.when(r == me_r)
        def _():
            rr[chunk] = value
            rrt[chunk] = stats

        @pl.when(r != me_r)
        def _():
            rs[r] = value
            rst[r] = stats
            remote(rs.at[r], rr.at[chunk], s_rs.at[0], s_rr.at[0], (r, me_t)).start()
            remote(rst.at[r], rrt.at[chunk], s_rs.at[1], s_rr.at[1], (r, me_t)).start()

    attend_short(yf)
    attend_new(3)
    for b in range(4):
        attend_local_end(b)

    await_bytes(rr.at[pl.ds(0, NREQ - 1)], s_rr.at[0])
    await_bytes(rrt.at[pl.ds(0, NREQ - 1)], s_rr.at[1])

    @pl.loop(0, 4)
    def _(n):
        b = (y + 1 + n) % NY
        at = rows_of(b, 256)
        lse = unpack_stats(rrt[pl.ds(b * 8, 8)])
        o = rr[pl.ds(b * 8, 8)].astype(F32).reshape(256, WIDE)
        m = m_l[at, :]
        top = jnp.maximum(m, lse)
        a, w = jnp.exp(m - top), jnp.exp(lse - top)
        value = (o_l[at, :] * a + o * w) / (l_l[at, :] * a + w)
        ctx[at, :] = value.astype(BF16)
        for i in range(2):
            to = b * 2 + i

            @pl.when(to != me_t)
            def _():
                remote(ctx.at[rows_of(to, 128), :], cr.at[me_t], s_cs, s_cr, (me_r, to)).start()

            @pl.when(to == me_t)
            def _():
                cr[me_t] = ctx[rows_of(to, 128), :]

    for step in range(4):
        gather_sibling(wo, s_wr, step)
    await_bytes(cr.at[pl.ds(0, NTP - 1)], s_cr)
    context = jnp.concatenate([cr[h] for h in range(NTP)], axis=1)
    attended = dot(context, wo[...].reshape(D, D)) + b_out[...]

    def norm(rows, which):
        center = rows - jnp.mean(rows, axis=-1, keepdims=True)
        var = jnp.mean(center * center, axis=-1, keepdims=True)
        return (center * lax.rsqrt(var + 1e-5) * gain[which : which + 1, :] + offset[which : which + 1, :]).astype(BF16)

    nrm[0] = norm(hid[me_t].astype(F32) + attended, 0)

    begin(nrm.at[0, top_half], nrm.at[1, top_half], s_ns.at[0], s_nr.at[0], right)
    begin(nrm.at[0, low_half], nrm.at[2, low_half], s_ns.at[2], s_nr.at[2], left)
    begin(nrm.at[0, low_half], nrm.at[1, low_half], s_ns.at[1], s_nr.at[1], right)
    begin(nrm.at[0, top_half], nrm.at[2, top_half], s_ns.at[3], s_nr.at[3], left)
    await_bytes(w1.at[1 - c], s_er.at[0])
    await_bytes(w2.at[1 - c], s_er.at[1])
    await_bytes(b1.at[1 - c], s_er.at[2])

    def feed(slot):
        rows = nrm[slot]
        total = None
        for i in range(2):
            u = dot(rows, w1[i]) + b1[i]
            u = (0.5 * u * (1.0 + lax.erf(u * 0.7071067811865476))).astype(BF16)
            term = dot(u, w2[i])
            total = term if total is None else total + term
        return total

    def piece(i):
        return pl.ds(i * (D // NP), D // NP)

    own_sum[...] = feed(0)
    await_bytes(nrm.at[1, top_half], s_nr.at[0])
    begin(nrm.at[1, top_half], nrm.at[3, top_half], s_ns.at[4], s_nr.at[4], right)
    await_bytes(nrm.at[2, low_half], s_nr.at[2])
    begin(nrm.at[2, low_half], nrm.at[3, low_half], s_ns.at[5], s_nr.at[5], left)
    await_bytes(nrm.at[1, low_half], s_nr.at[1])
    part[1] = feed(1).astype(BF16)
    begin(part.at[1, top_half], fr.at[top_half], s_fs.at[0], s_fr.at[0], left)
    await_bytes(nrm.at[2, top_half], s_nr.at[3])
    part[2] = feed(2).astype(BF16)
    begin(part.at[2, low_half], fl.at[low_half], s_fs.at[1], s_fr.at[1], right)
    await_bytes(nrm.at[3, top_half], s_nr.at[4])
    await_bytes(nrm.at[3, low_half], s_nr.at[5])
    part[3] = feed(3).astype(BF16)
    for i in range(NP):
        begin(part.at[3, top_half, piece(i)], ra.at[:, piece(i)], s_fs.at[2 + 4 * i], s_fr.at[2 + 4 * i], right)
        begin(part.at[3, low_half, piece(i)], rb.at[:, piece(i)], s_fs.at[3 + 4 * i], s_fr.at[3 + 4 * i], left)
    for i in range(NP):
        at = piece(i)
        await_bytes(ra.at[:, at], s_fr.at[2 + 4 * i])
        part[2, 0:64, at] = (part[2, 0:64, at].astype(F32) + ra[:, at].astype(F32)).astype(BF16)
        begin(part.at[2, top_half, at], fl.at[top_half, at], s_fs.at[4 + 4 * i], s_fr.at[4 + 4 * i], right)
        await_bytes(rb.at[:, at], s_fr.at[3 + 4 * i])
        part[1, 64:128, at] = (part[1, 64:128, at].astype(F32) + rb[:, at].astype(F32)).astype(BF16)
        begin(part.at[1, low_half, at], fr.at[low_half, at], s_fs.at[5 + 4 * i], s_fr.at[5 + 4 * i], left)
    await_bytes(fr.at[top_half], s_fr.at[0])
    await_bytes(fl.at[low_half], s_fr.at[1])
    for i in range(NP):
        await_bytes(fl.at[top_half, piece(i)], s_fr.at[4 + 4 * i])
        await_bytes(fr.at[low_half, piece(i)], s_fr.at[5 + 4 * i])
    mixed = own_sum[...] + fl[...].astype(F32) + fr[...].astype(F32) + b_down[...]
    out_ref[...] = norm(nrm[0].astype(F32) + mixed, 1)

    for copy in sent:
        copy.wait_send()
    await_bytes(qa.at[pl.ds(0, NREQ - 1)], s_qas)
    await_bytes(qz.at[pl.ds(1, NZ - 1)], s_qzs)
    for j in range(NLONG):
        await_bytes(pr.at[j, pl.ds(1, NZ - 1)], s_ps.at[j])
        await_bytes(prt.at[j, pl.ds(1, NZ - 1)], s_ps.at[3 + j])
    await_bytes(rr.at[pl.ds(0, NREQ - 1)], s_rs.at[0])
    await_bytes(rrt.at[pl.ds(0, NREQ - 1)], s_rs.at[1])
    await_bytes(cr.at[pl.ds(0, NTP - 1)], s_cs)
    out_copy.wait()


def body(
    hidden_in, short_cache, long_cache, short_len, long_owner, w_qkv, b_qkv, w_out, b_out,
    w_in, b_in, w_down, b_down, norm_gain, norm_offset,
):
    hbm = pl.BlockSpec(memory_space=pl.ANY)
    vmem = pl.BlockSpec(memory_space=pltpu.VMEM)
    smem = pl.BlockSpec(memory_space=pltpu.SMEM)
    V, S = pltpu.VMEM, pltpu.SemaphoreType.DMA
    hidden_out, new_kv = pl.pallas_call(
        kernel,
        out_shape=(
            jax.ShapeDtypeStruct((128, D), BF16),
            jax.ShapeDtypeStruct((2 * SPAN, WIDE), BF16),
        ),
        in_specs=[
            hbm, hbm, hbm, smem, smem, hbm, vmem, hbm, vmem, hbm, hbm, hbm, vmem, vmem, vmem,
        ],
        out_specs=(vmem, hbm),
        scratch_shapes=[
            V((NTP, 128, D), BF16),
            V((D, 3 * WIDE), BF16),
            V((2 * SHORT, WIDE), BF16),
            V((NX, 2 * NLONG * LSEG, WIDE), BF16),
            V((NTP, WIDE, D), BF16),
            V((2, D, FFH), BF16),
            V((2, FFH, D), BF16),
            V((2, 1, FFH), F32),
            V((SPAN, WIDE), BF16),
            V((SHORT + SPAN, WIDE), BF16),
            V((SHORT + SPAN, WIDE), BF16),
            V((NLONG, NX * LSEG, WIDE), BF16),
            V((NLONG, NX * LSEG, WIDE), BF16),
            V((NREQ, CH, WIDE), BF16),
            V((NLONG, CH, WIDE), BF16),
            V((NZ, NLONG, CH, WIDE), BF16),
            V((8, SHORT), F32),
            V((256, 256), BF16),
            V((256, 256), BF16),
            V((4, 2, 256, WIDE), F32),
            V((4, 2, 256, WIDE), F32),
            V((2, 256, WIDE), F32),
            V((2, 256, WIDE), F32),
            V((SPAN, WIDE), F32),
            V((SPAN, WIDE), F32),
            V((SPAN, WIDE), F32),
            V((NLONG, NZ, CH, WIDE), BF16),
            V((NLONG, NZ, CH, WIDE), BF16),
            V((NLONG, NZ, 1, WIDE), F32),
            V((NLONG, NZ, 1, WIDE), F32),
            V((NLONG, CH, WIDE), F32),
            V((NLONG, 1, WIDE), F32),
            V((NREQ, CH, WIDE), BF16),
            V((NREQ, CH, WIDE), BF16),
            V((NREQ, 1, WIDE), F32),
            V((NREQ, 1, WIDE), F32),
            V((SPAN, WIDE), BF16),
            V((NTP, 128, WIDE), BF16),
            V((NY, 128, D), BF16),
            V((NY, 128, D), BF16),
            V((128, D), F32),
            V((64, D), BF16),
            V((64, D), BF16),
            V((128, D), BF16),
            V((128, D), BF16),
            V((2 * SPAN, WIDE), BF16),
            S((10,)), S((12,)), S((12,)), S((12,)), S((12,)), S((12,)), S((12,)), S((3,)), S((3,)),
            S, S, S, S, S((6,)), S((6,)), S((2,)), S((2,)), S, S, S((6,)), S((6,)),
            S((2 + 4 * NP,)), S((2 + 4 * NP,)), S((1,)),
        ],
        compiler_params=pltpu.CompilerParams(
            collective_id=0, has_side_effects=True, vmem_limit_bytes=56 * 1024 * 1024
        ),
    )(
        hidden_in[0],
        short_cache.reshape(2 * SHORT, WIDE),
        long_cache.reshape(2 * NLONG * LSEG, WIDE),
        short_len,
        long_owner,
        w_qkv,
        b_qkv,
        w_out,
        b_out[None],
        w_in,
        b_in[None],
        w_down,
        b_down[None],
        norm_gain,
        norm_offset,
    )
    return (hidden_out[None], new_kv.reshape(1, SPAN, 2, WIDE))


def solution(mesh):
    return jax.shard_map(
        body,
        mesh=mesh,
        in_specs=(
            P("req", "tp", None),
            P("req", None, None, "tp"),
            P(None, "req", None, "tp"),
            P("req"),
            P(),
            P(None, None, "tp"),
            P(None, "tp"),
            P("tp", None),
            P(),
            P(None, "tp"),
            P("tp"),
            P("tp", None),
            P(),
            P(),
            P(),
        ),
        out_specs=(P("req", "tp", None), P("req", None, None, "tp")),
        check_vma=False,
    )
```
